1024 devices in a mesh: dp: 128 (over y, z), fsdp: 8 (over x, core).
Axes of the slice: x: 4, y: 8, z: 16, core: 2. Of those that a mesh axis runs over, the one named last changes fastest.
Arguments:
- crops: bfloat16 [1024, 4, 8, 8, 256], P(('dp', 'fsdp')), may hold values from -6 to 6
- weight: bfloat16 [256, 27, 128], P('fsdp'), may hold values from -0.078125 to 0.078125
- bucket_bias: float32 [8, 128], replicated, may hold values from -4 to 4
- norm_gain: float32 [128], replicated, may hold values from 0.25 to 1.75
- norm_shift: float32 [128], replicated, may hold values from -3 to 3
- bucket_ids: int32 [1024], P(('dp', 'fsdp')), may hold values from 0 to 7
- valid_counts: int32 [1024], P(('dp', 'fsdp')), may hold values from 64 to 256
- cotangent: bfloat16 [1024, 256, 128], P(('dp', 'fsdp')), may hold values from -0.011962891 to 0.011962891
Outputs:
- activated: bfloat16 [1024, 256, 128], P(('dp', 'fsdp'))
- weight_grad: float32 [256, 27, 128], P('fsdp')
The draws below stay inside these ranges and needn't reach their ends.
All inputs are finite; a program needn't handle non-finite values.
Results may differ from the reference program's by a relative error of at most 0.0029.
Values may be sent and summed in bfloat16 or wider, within the bound.
A program may use at most 32 MiB of HBM per device.

```python
import jax
import jax.numpy as jnp
from jax import lax

CIN = 256
COUT = 128
GSIZE = 8
TAPS = 27
BUCKETS = 8
DZ = 4
DY = 8
DX = 8
VOX = 256
CROPS = 1024


def place_ends(values, key, least, high):
    index_at = [jax.random.randint(jax.random.fold_in(key, axis), (), 0, length) for axis, length in enumerate(values.shape)]
    widest = values.shape.index(max(values.shape))
    beside = index_at[:widest] + [(index_at[widest] + 1) % values.shape[widest]] + index_at[widest + 1:]
    return values.at[tuple(index_at)].set(least).at[tuple(beside)].set(high)


def shard_levels(key, shape, split, smallest, high):
    level = 1.0
    for dim, shards_of in split:
        heights = jax.random.uniform(jax.random.fold_in(jax.random.fold_in(key, 6), dim), (shards_of,), jnp.float32, smallest / len(split), high / len(split))
        level = level * jnp.repeat(jnp.exp(heights), shape[dim] // shards_of).reshape((-1,) + (1,) * (len(shape) - 1 - dim))
    return level


def bell_draw(rng, shape, width, limit, shards=(), held_as=jnp.bfloat16):
    values = jax.random.normal(rng, shape, jnp.float32) * width
    if len(shards) > 0:
        values = shard_levels(rng, shape, shards, -0.22, 0.18) * values
    return jnp.clip(values, min=-limit, max=limit).astype(held_as)


def setup_inputs(seed: int = 0) -> dict:
    splits = jax.random.split(jax.random.key(seed), 9)
    crops = bell_draw(splits[0], (CROPS, DZ, DY, DX, CIN), 1.0, 6.0, ((0, 1024),))
    weight = bell_draw(splits[1], (CIN, TAPS, COUT), (CIN * TAPS) ** -0.5, 0.078125, ((0, 8),))
    bucket_bias = bell_draw(splits[2], (BUCKETS, COUT), 1.0, 4.0, (), jnp.float32)
    norm_gain = jnp.clip(1.0 + 0.15 * jax.random.normal(splits[3], (COUT,), jnp.float32), 0.25, 1.75)
    norm_shift = bell_draw(splits[4], (COUT,), 0.5, 3.0, (), jnp.float32)
    bucket_ids = place_ends(jax.random.randint(splits[5], (CROPS,), 0, BUCKETS), jax.random.fold_in(splits[5], 1), 0, BUCKETS - 1).astype(jnp.int32)
    valid_counts = place_ends(jax.random.randint(splits[6], (CROPS,), VOX // 4, VOX + 1), jax.random.fold_in(splits[6], 1), VOX // 4, VOX).astype(jnp.int32)
    cotangent = bell_draw(splits[7], (CROPS, VOX, COUT), 0.002, 0.011962891, ((0, 1024),))
    return {"crops": crops, "weight": weight, "bucket_bias": bucket_bias, "norm_gain": norm_gain, "norm_shift": norm_shift, "bucket_ids": bucket_ids, "valid_counts": valid_counts, "cotangent": cotangent}


epsilon = 1e-05

def normalize(pre_norm, mask_col, count, gain, shift, bias_row):
    voxels, chans = pre_norm.shape
    grouped = pre_norm.reshape(voxels, chans // GSIZE, GSIZE)
    weights = mask_col[:, :, None]
    entries = count.astype(jnp.float32) * GSIZE
    mean_val = lax.optimization_barrier(jnp.sum(grouped * weights, axis=(0, 2))) / entries
    centered = grouped - mean_val[None, :, None]
    var_val = lax.optimization_barrier(jnp.sum(centered * centered * weights, axis=(0, 2))) / entries
    normed = (centered * lax.rsqrt(var_val + epsilon)[None, :, None]).reshape(voxels, chans)
    return jax.nn.silu(normed * gain + shift + bias_row) * mask_col

def reference(crops, weight, bucket_bias, norm_gain, norm_shift, bucket_ids, valid_counts, cotangent):

    def crop_step(total, inputs):
        volume, bucket, count, upstream = inputs
        mask_col = (jnp.arange(VOX) < count).astype(jnp.float32)[:, None]
        masked = (volume.astype(jnp.float32) * mask_col.reshape(DZ, DY, DX, 1)).astype(jnp.bfloat16)
        padded = jnp.pad(masked, ((1, 1), (1, 1), (1, 1), (0, 0)))
        slabs = []
        for tap_index in range(27):
            depth_off = tap_index // 9
            row_off = tap_index // 3 % 3
            col_off = tap_index % 3
            slabs.append(padded[depth_off:depth_off + DZ, row_off:row_off + DY, col_off:col_off + DX, :].reshape(VOX, CIN))
        pre_norm = jnp.zeros((VOX, COUT), jnp.float32)
        for tap_index in range(27):
            pre_norm = pre_norm + jnp.dot(slabs[tap_index], weight[:, tap_index, :], preferred_element_type=jnp.float32)
        bias_row = lax.optimization_barrier(jnp.sum(jnp.where(jnp.arange(BUCKETS)[:, None] == bucket, bucket_bias, 0.0), axis=0))
        outputs, pullback = jax.vjp(lambda value: normalize(value, mask_col, count, norm_gain, norm_shift, bias_row), pre_norm)
        grad_pre = pullback(upstream.astype(jnp.float32))[0].astype(jnp.bfloat16)
        terms = [lax.dot_general(slab, grad_pre, (((0,), (0,)), ((), ())), preferred_element_type=jnp.float32) for slab in slabs]
        return (total + jnp.stack(terms, axis=1), outputs.astype(jnp.bfloat16))
    start_total = jnp.zeros((CIN, TAPS, COUT), jnp.float32)
    weight_grad, activated = lax.scan(crop_step, start_total, (crops, bucket_ids, valid_counts, cotangent))
    return (activated, weight_grad)
```

```python
import functools

import jax
import jax.numpy as jnp
from jax import lax
from jax.experimental import pallas as pl
from jax.experimental.pallas import tpu as pltpu
from jax.sharding import PartitionSpec as P

MESH = pl.DeviceIdType.MESH
F32 = jnp.float32
BF16 = jnp.bfloat16

EPSILON = 1e-05
VOX = 256
OWN = 32
OUTS = 128
QUARTER = 32
TAPS = 27
TILES = 7
COLS = TILES * 128
UNITS = 16
REAL = 2 * TILES
CHUNKS = ((0, 256), (256, 256), (512, 256), (768, 128))


def lane_fields():
    lane = lax.broadcasted_iota(jnp.int32, (8, VOX), 1)
    return lane >> 6, (lane >> 3) & 7, lane & 7


def inside(offset, field, cells):
    moved = field + offset
    return jnp.logical_and(moved >= 0, moved < cells)[0:1]


def wait_bytes(ref, sem):
    pltpu.make_async_copy(ref, ref, sem).wait()


def kernel(
    geometry,
    count_ref, bucket_ref, crop_ref, weight_ref, bias_ref, gain_ref, shift_ref, cot_ref,
    act_ref, grad_ref,
    x_ref, xt_ref, wf_ref, wg_ref, wt_ref, ct_ref, c4_ref, meta_ref, par_ref,
    g_ref, dwf_ref, d1s_ref, d1r_ref, s_ref, r2_ref, f_ref, acts_ref, actr_ref,
    w_send, w_recv, x_send, x_recv, c_send, c_recv, m_send, m_recv, a_send, a_recv,
    d1_send, d1_recv, d2_send, d2_recv, e1_send, e1_recv, e2_send, e2_recv,
):
    ny, nz, peers = geometry
    nyp, nzp = ny // 2, nz // 2
    per_row = UNITS // nyp
    per_dev = max(1, per_row // nzp)
    stride = max(1, nzp // per_row)
    chans = OWN * peers

    dp = lax.axis_index("dp")
    fs = lax.axis_index("fsdp")
    y, z = dp // nz, dp % nz
    yp, zp, qy, qz = y // 2, z // 2, y % 2, z % 2
    q = qy * 2 + qz

    def plane(yy, zz):
        return (yy * nz + zz, fs)

    def along(k):
        return (dp, lax.rem(fs + k, peers))

    def member(k):
        return plane(2 * yp + (qy ^ (k >> 1)), 2 * zp + (qz ^ (k & 1)))

    barrier = pltpu.get_barrier_semaphore()

    def greet(device):
        pl.semaphore_signal(barrier, inc=1, device_id=device, device_id_type=MESH)

    for k in range(1, peers):
        greet(along(k))
    for k in range(1, 4):
        greet(member(k))
    greeted = peers - 1 + 3

    @pl.loop(1, nyp * nzp)
    def _(i):
        yy = lax.rem(yp + i // nzp, nyp)
        zz = lax.rem(zp + i % nzp, nzp)
        greet(plane(2 * yy + qy, 2 * zz + qz))

    greeted += nyp * nzp - 1
    for k in range(1, nzp):
        greet(plane(y, 2 * lax.rem(zp + k, nzp) + 1 - qz))
    for k in range(1, nyp):
        greet(plane(2 * lax.rem(yp + k, nyp) + 1 - qy, z))
    greeted += nzp - 1 + nyp - 1

    count = count_ref[0]
    bucket = bucket_ref[0]
    rows = lax.broadcasted_iota(jnp.int32, (VOX, 1), 0)
    row_mask = (rows < count).astype(F32)
    x_ref[0] = (crop_ref[...].astype(F32) * row_mask).astype(BF16)

    for c in range(OWN):
        wf_ref[pl.ds(32 * c, TAPS), :] = weight_ref[c].astype(F32)
    lane_block = lax.broadcasted_iota(jnp.int32, (OWN, 128), 1) >> 5
    mine = pl.ds(pl.multiple_of(OWN * fs, OWN), OWN)
    for g in range(TILES):
        tile = jnp.zeros((OWN, 128), F32)
        for j in range(4):
            if 4 * g + j < TAPS:
                tap = wf_ref[pl.ds(4 * g + j, OWN, stride=32), :]
                tap = pltpu.roll(tap, lax.rem(32 * (j - q) + 128, 128), 1)
                tile = jnp.where(lane_block == j, tap, tile)
        wg_ref[mine, pl.ds(128 * g, 128)] = tile.astype(BF16)

    ct_ref[...] = cot_ref[...].astype(F32).T.astype(BF16)
    bias_rows = lax.broadcasted_iota(jnp.int32, (8, OUTS), 0)
    bias_row = jnp.sum(jnp.where(bias_rows == bucket, bias_ref[...], 0.0), axis=0, keepdims=True)
    meta_ref[0] = jnp.where(bias_rows == 0, bias_row, count.astype(F32))

    pl.semaphore_wait(barrier, greeted)

    w_copies = []
    for k in range(1, peers):
        copy = pltpu.make_async_remote_copy(
            src_ref=wg_ref.at[mine, :], dst_ref=wg_ref.at[mine, :],
            send_sem=w_send.at[k - 1], recv_sem=w_recv, device_id=along(k), device_id_type=MESH,
        )
        copy.start()
        w_copies.append(copy)
    block_copies = []
    for k in range(1, 4):
        to = pl.ds(pl.multiple_of(QUARTER * (q ^ k), QUARTER), QUARTER)
        for src, dst, send, recv in (
            (meta_ref.at[0], meta_ref.at[k], m_send, m_recv),
            (ct_ref.at[to, :], c4_ref.at[k], c_send, c_recv),
            (x_ref.at[0], x_ref.at[k], x_send, x_recv),
        ):
            copy = pltpu.make_async_remote_copy(
                src_ref=src, dst_ref=dst, send_sem=send.at[k - 1], recv_sem=recv.at[k - 1],
                device_id=member(k), device_id_type=MESH,
            )
            copy.start()
            block_copies.append(copy)
    quarter = pl.ds(pl.multiple_of(QUARTER * q, QUARTER), QUARTER)
    c4_ref[0] = ct_ref[quarter, :]

    for k in range(1, 4):
        wait_bytes(meta_ref.at[k], m_recv.at[k - 1])
    table = jnp.concatenate(
        [meta_ref[k, 0:1, :] for k in range(4)]
        + [gain_ref[...], shift_ref[...], jnp.zeros((122, OUTS), F32)],
        axis=0,
    )
    par_ref[...] = table.T
    params = par_ref[quarter, :]
    param_lane = lax.broadcasted_iota(jnp.int32, (QUARTER, OUTS), 1)

    def column(index):
        return jnp.sum(jnp.where(param_lane == index, params, 0.0), axis=1, keepdims=True)

    gain = column(4)
    shift = column(5)

    if peers > 1:
        wait_bytes(wg_ref.at[pl.ds(0, OWN * (peers - 1)), :], w_recv)
    for g in range(TILES):
        wt_ref[pl.ds(128 * g, 128), :] = wg_ref[:, pl.ds(128 * g, 128)].astype(F32).T.astype(BF16)

    zf, yf, xf = lane_fields()
    reach = {
        (axis, offset): inside(offset, field, cells).astype(F32)
        for axis, field, cells in (("z", zf, 4), ("y", yf, 8), ("x", xf, 8))
        for offset in (-1, 1)
    }

    def moved(value, axis, offset, step):
        if offset == 0:
            return value
        rolled = pltpu.roll(value, (-offset * step) % VOX, 1)
        return rolled * reach[axis, offset]

    def group_sum(value):
        grouped = value.reshape(QUARTER // 8, 8, VOX)
        total = jnp.sum(jnp.sum(grouped, axis=2, keepdims=True), axis=1, keepdims=True)
        return total

    def per_crop(m, carry):
        @pl.when(m > 0)
        def _():
            wait_bytes(x_ref.at[m], x_recv.at[m - 1])
            wait_bytes(c4_ref.at[m], c_recv.at[m - 1])

        xt = x_ref[m].astype(F32).T.astype(BF16)
        xt_ref[m] = xt
        pre = jnp.zeros((QUARTER, VOX), F32)
        sum_z = sum_y = None
        for g in range(TILES):
            product = jnp.dot(wt_ref[pl.ds(128 * g, 128), :], xt, preferred_element_type=F32)
            for j in range(4):
                t = 4 * g + j
                if t >= TAPS:
                    continue
                a, b, e = t // 9 - 1, t // 3 % 3 - 1, t % 3 - 1
                part = moved(product[32 * j : 32 * j + 32], "x", e, 1)
                sum_y = part if e == -1 else sum_y + part
                if e == 1:
                    part = moved(sum_y, "y", b, 8)
                    sum_z = part if b == -1 else sum_z + part
                    if b == 1:
                        pre = pre + moved(sum_z, "z", a, 64)

        cells = meta_ref[m][1:2, 0:1]
        lane = lax.broadcasted_iota(jnp.int32, (1, VOX), 1).astype(F32)
        mask = (lane < cells).astype(F32)
        inverse = 1.0 / (cells * 8.0)
        inverse = inverse.reshape(1, 1, 1)

        def spread(total):
            return jnp.broadcast_to(total, (QUARTER // 8, 8, VOX)).reshape(QUARTER, VOX)

        mean = spread(group_sum(pre * mask) * inverse)
        centered = pre - mean
        variance = group_sum(centered * centered * mask) * inverse
        scale = spread(lax.rsqrt(variance + EPSILON))
        normed = centered * scale
        value = normed * gain + shift + column(m)
        sig = 1.0 / (1.0 + jnp.exp(-value))
        acts_ref[m] = (value * sig * mask).astype(BF16)
        d_normed = c4_ref[m].astype(F32) * mask * (sig * (1.0 + value * (1.0 - sig))) * gain
        mean_d = spread(group_sum(d_normed) * inverse)
        mean_dn = spread(group_sum(d_normed * normed) * inverse)
        grad = scale * (d_normed - mask * (mean_d + normed * mean_dn))
        grad = grad.astype(BF16).astype(F32)
        for a in range(-1, 2):
            grad_a = moved(grad, "z", -a, 64)
            for b in range(-1, 2):
                grad_ab = moved(grad_a, "y", -b, 8)
                for e in range(-1, 2):
                    t = 9 * (a + 1) + 3 * (b + 1) + e + 1
                    g_ref[m, pl.ds(32 * t, 32), :] = moved(grad_ab, "x", -e, 1).astype(BF16)
        g_ref[m, pl.ds(32 * TAPS, 32), :] = jnp.zeros((32, VOX), BF16)
        return carry

    lax.fori_loop(0, 4, per_crop, 0)

    act_copies = []
    for k in range(1, 4):
        copy = pltpu.make_async_remote_copy(
            src_ref=acts_ref.at[k], dst_ref=actr_ref.at[quarter, :],
            send_sem=a_send.at[k - 1], recv_sem=a_recv.at[k - 1],
            device_id=member(k), device_id_type=MESH,
        )
        copy.start()
        act_copies.append(copy)
    actr_ref[quarter, :] = acts_ref[0]

    d1_copies = []
    for index, (start, width) in enumerate(CHUNKS):
        lanes = pl.ds(start, width)
        total = jnp.zeros((chans, width), F32)
        for m in range(4):
            total = total + lax.dot_general(
                xt_ref[m], g_ref[m, lanes, :], (((1,), (1,)), ((), ())), preferred_element_type=F32
            )
        dwf_ref[:, lanes] = total
        d1s_ref[:, lanes] = total.astype(BF16)
        for k in range(1, peers):
            theirs = pl.ds(pl.multiple_of(OWN * lax.rem(fs + k, peers), OWN), OWN)
            copy = pltpu.make_async_remote_copy(
                src_ref=d1s_ref.at[theirs, lanes], dst_ref=d1r_ref.at[k - 1, :, lanes],
                send_sem=d1_send.at[index], recv_sem=d1_recv.at[index],
                device_id=along(k), device_id_type=MESH,
            )
            copy.start()
            d1_copies.append(copy)

    def owner(u):
        place = u % per_row
        if per_dev > 1:
            return u // per_row, place // per_dev
        return u // per_row, place * stride

    d2_copies = []
    for index, (start, width) in enumerate(CHUNKS):
        lanes = pl.ds(start, width)
        if peers > 1:
            wait_bytes(d1r_ref.at[:, :, lanes], d1_recv.at[index])
        total = dwf_ref[mine, lanes]
        for k in range(1, peers):
            total = total + d1r_ref[k - 1, :, lanes].astype(F32)
        for g in range(start // 128, (start + width) // 128):
            for h in range(2):
                u = 2 * g + h
                at = 128 * g - start
                s_ref[u] = total[16 * h : 16 * h + 16, at : at + 128]
                oy, oz = owner(u)
                away = jnp.logical_or(yp != oy, zp != oz)
                slot = lax.rem(yp - oy + nyp, nyp) * nzp + lax.rem(zp - oz + nzp, nzp) - 1
                copy = pltpu.make_async_remote_copy(
                    src_ref=s_ref.at[u],
                    dst_ref=r2_ref.at[u % per_dev, jnp.maximum(slot, 0)],
                    send_sem=d2_send.at[u], recv_sem=d2_recv.at[u % per_dev],
                    device_id=plane(2 * oy + qy, 2 * oz + qz), device_id_type=MESH,
                )
                pl.when(away)(copy.start)
                d2_copies.append((away, copy))

    if per_dev > 1:
        owns = yp >= 0
        first = yp * per_row + zp * per_dev
    else:
        owns = lax.rem(zp, stride) == 0
        first = yp * per_row + zp // stride

    def row_peer(k):
        return plane(y, lax.rem(z + k, nz))

    def place_of(u):
        return lax.rem(u, per_row)

    @pl.when(owns)
    def _():
        for i in range(per_dev):
            u = first + i

            @pl.when(u < REAL)
            def _():
                wait_bytes(r2_ref.at[i], d2_recv.at[i])
                total = s_ref[u]
                for k in range(nyp * nzp - 1):
                    total = total + r2_ref[i, k]
                f_ref[u, qy, qz] = total.astype(BF16)

            @pl.when(u >= REAL)
            def _():
                f_ref[u, qy, qz] = jnp.zeros((16, 128), BF16)

            for k in range(1, nz):
                pltpu.make_async_remote_copy(
                    src_ref=f_ref.at[u, qy, qz], dst_ref=f_ref.at[u, qy, qz],
                    send_sem=e1_send.at[i, k - 1], recv_sem=e1_recv.at[place_of(u), qz],
                    device_id=row_peer(k), device_id_type=MESH,
                ).start()

    for k in range(1, 4):
        theirs = pl.ds(pl.multiple_of(QUARTER * (q ^ k), QUARTER), QUARTER)
        wait_bytes(actr_ref.at[theirs, :], a_recv.at[k - 1])
    act_ref[...] = actr_ref[...].astype(F32).T.astype(BF16)

    for place in range(per_row):
        u = yp * per_row + place
        for side in range(2):
            if per_dev > 1:
                local = jnp.logical_and(zp == place // per_dev, qz == side)
            else:
                local = jnp.logical_and(zp == place * stride, qz == side)

            @pl.when(jnp.logical_not(local))
            def _():
                wait_bytes(f_ref.at[u, qy, side], e1_recv.at[place, side])

    row_units = f_ref.at[pl.ds(pl.multiple_of(yp * per_row, per_row), per_row), qy]
    e2_copies = []
    for k in range(1, ny):
        copy = pltpu.make_async_remote_copy(
            src_ref=row_units, dst_ref=row_units,
            send_sem=e2_send.at[k - 1], recv_sem=e2_recv.at[k - 1],
            device_id=plane(lax.rem(y + k, ny), z), device_id_type=MESH,
        )
        copy.start()
        e2_copies.append(copy)
    for copy in e2_copies:
        copy.wait_recv()

    block16 = lax.broadcasted_iota(jnp.int32, (16, 128), 1) >> 5
    for g in range(TILES):
        for h in range(2):
            quarters = [f_ref[2 * g + h, p // 2, p % 2].astype(F32) for p in range(4)]
            for j in range(4):
                t = 4 * g + j
                if t >= TAPS:
                    continue
                line = jnp.zeros((16, 128), F32)
                for p in range(4):
                    turned = quarters[p] if p == j else pltpu.roll(quarters[p], (32 * (p - j)) % 128, 1)
                    line = jnp.where(block16 == p, turned, line)
                grad_ref[pl.ds(16 * h * 32 + t, 16, stride=32), :] = line
    for c in range(OWN):
        grad_ref[pl.ds(32 * c + TAPS, 32 - TAPS), :] = jnp.zeros((32 - TAPS, 128), F32)

    for copy in w_copies + block_copies + act_copies + e2_copies:
        copy.wait_send()
    if peers > 1:
        for index, (start, width) in enumerate(CHUNKS):
            wait_bytes(d1r_ref.at[:, :, pl.ds(start, width)], d1_send.at[index])
    for away, copy in d2_copies:
        pl.when(away)(copy.wait_send)

    @pl.when(owns)
    def _():
        for i in range(per_dev):
            for k in range(1, nz):
                wait_bytes(f_ref.at[first + i, qy, qz], e1_send.at[i, k - 1])


def body(geometry, crops, weight, bucket_bias, norm_gain, norm_shift, bucket_ids, valid_counts, cotangent):
    ny, nz, peers = geometry
    nyp, nzp = ny // 2, nz // 2
    per_row = UNITS // nyp
    per_dev = max(1, per_row // nzp)
    chans = OWN * peers
    others = max(1, peers - 1)
    smem = pl.BlockSpec(memory_space=pltpu.SMEM)
    vmem = pl.BlockSpec(memory_space=pltpu.VMEM)
    dma = pltpu.SemaphoreType.DMA
    activated, grad = pl.pallas_call(
        functools.partial(kernel, geometry),
        out_shape=(
            jax.ShapeDtypeStruct((VOX, OUTS), BF16),
            jax.ShapeDtypeStruct((OWN * 32, OUTS), F32),
        ),
        in_specs=[smem, smem] + [vmem] * 6,
        out_specs=(vmem, vmem),
        scratch_shapes=[
            pltpu.VMEM((4, VOX, chans), BF16),
            pltpu.VMEM((4, chans, VOX), BF16),
            pltpu.VMEM((OWN * 32, OUTS), F32),
            pltpu.VMEM((chans, COLS), BF16),
            pltpu.VMEM((COLS, chans), BF16),
            pltpu.VMEM((OUTS, VOX), BF16),
            pltpu.VMEM((4, QUARTER, VOX), BF16),
            pltpu.VMEM((4, 8, OUTS), F32),
            pltpu.VMEM((OUTS, OUTS), F32),
            pltpu.VMEM((4, COLS, VOX), BF16),
            pltpu.VMEM((chans, COLS), F32),
            pltpu.VMEM((chans, COLS), BF16),
            pltpu.VMEM((others, OWN, COLS), BF16),
            pltpu.VMEM((REAL, 16, 128), F32),
            pltpu.VMEM((per_dev, nyp * nzp - 1, 16, 128), F32),
            pltpu.VMEM((UNITS, 2, 2, 16, 128), BF16),
            pltpu.VMEM((4, QUARTER, VOX), BF16),
            pltpu.VMEM((OUTS, VOX), BF16),
            dma((others,)), dma,
            dma((3,)), dma((3,)),
            dma((3,)), dma((3,)),
            dma((3,)), dma((3,)),
            dma((3,)), dma((3,)),
            dma((len(CHUNKS),)), dma((len(CHUNKS),)),
            dma((REAL,)), dma((per_dev,)),
            dma((per_dev, nz - 1)), dma((per_row, 2)),
            dma((ny - 1,)), dma((ny - 1,)),
        ],
        compiler_params=pltpu.CompilerParams(
            collective_id=0, has_side_effects=True, vmem_limit_bytes=40 * 1024 * 1024
        ),
    )(
        valid_counts, bucket_ids,
        crops.reshape(VOX, chans), weight, bucket_bias,
        norm_gain.reshape(1, OUTS), norm_shift.reshape(1, OUTS), cotangent.reshape(VOX, OUTS),
    )
    weight_grad = grad.reshape(OWN, 32, OUTS)[:, :TAPS, :]
    return activated[None], weight_grad


def solution(mesh):
    chips = mesh.shape["dp"]
    ny = 8 if chips == 128 else 2
    geometry = (ny, chips // ny, mesh.shape["fsdp"])
    return jax.shard_map(
        functools.partial(body, geometry),
        mesh=mesh,
        in_specs=(
            P(("dp", "fsdp"), None, None, None, None),
            P("fsdp", None, None),
            P(),
            P(),
            P(),
            P(("dp", "fsdp")),
            P(("dp", "fsdp")),
            P(("dp", "fsdp"), None, None),
        ),
        out_specs=(P(("dp", "fsdp"), None, None), P("fsdp", None, None)),
        check_vma=False,
    )
```

```python
import functools

import jax
import jax.numpy as jnp
from jax import lax
from jax.experimental import pallas as pl
from jax.experimental.pallas import tpu as pltpu
from jax.sharding import PartitionSpec as P

MESH = pl.DeviceIdType.MESH
F32 = jnp.float32
BF16 = jnp.bfloat16

EPSILON = 1e-05
VOX = 256
OWN = 32
OUTS = 128
QUARTER = 32
TAPS = 27
TILES = 7
COLS = TILES * 128
UNITS = 16
REAL = 2 * TILES
CHUNKS = ((0, 256), (256, 256), (512, 256), (768, 128))


def lane_fields():
    lane = lax.broadcasted_iota(jnp.int32, (8, VOX), 1)
    return lane >> 6, (lane >> 3) & 7, lane & 7


def inside(offset, field, cells):
    moved = field + offset
    return jnp.logical_and(moved >= 0, moved < cells)[0:1]


def wait_bytes(ref, sem):
    pltpu.make_async_copy(ref, ref, sem).wait()


def kernel(
    geometry,
    count_ref, bucket_ref, crop_hbm, weight_hbm, bias_hbm, gain_hbm, shift_hbm, cot_hbm,
    act_ref, grad_ref,
    crop_ref, weight_ref, bias_ref, gain_ref, shift_ref, cot_ref, in_sem,
    x_ref, xt_ref, wg_ref, wt_ref, ct_ref, c4_ref, meta_ref, par_ref,
    g_ref, dwf_ref, d0r_ref, d1s_ref, d1r_ref, s_ref, r2_ref, f_ref, acts_ref, actr_ref,
    told, w_send, w_recv, x_send, x_recv, c_send, c_recv, m_send, m_recv, a_send, a_recv,
    d0_send, d0_recv, d1_send, d1_recv, d2_send, d2_recv, e1_send, e1_recv, e2_send, e2_recv,
):
    ny, nz, peers = geometry
    nyp, nzp = ny // 2, nz // 2
    per_row = UNITS // nyp
    spots = min(per_row, nzp, 4)
    per_dev = per_row // spots
    chans = OWN * peers

    dp = lax.axis_index("dp")
    fs = lax.axis_index("fsdp")
    y, z = dp // nz, dp % nz
    yp, zp, qy, qz = y // 2, z // 2, y % 2, z % 2
    q = qy * 2 + qz

    def plane(yy, zz):
        return (yy * nz + zz, fs)

    def along(k):
        return (dp, lax.rem(fs + k, peers))

    def member(k):
        return plane(2 * yp + (qy ^ (k >> 1)), 2 * zp + (qz ^ (k & 1)))

    loads = [
        pltpu.make_async_copy(src, dst, in_sem.at[index])
        for index, (src, dst) in enumerate((
            (crop_hbm, crop_ref), (weight_hbm, weight_ref), (cot_hbm, cot_ref),
            (bias_hbm, bias_ref), (gain_hbm, gain_ref), (shift_hbm, shift_ref),
        ))
    ]
    for load in loads:
        load.start()

    barrier = pltpu.get_barrier_semaphore()

    def greet(device):
        pl.semaphore_signal(barrier, inc=1, device_id=device, device_id_type=MESH)

    for k in range(1, peers):
        greet(along(k))
    for k in range(1, 4):
        greet(member(k))
    greeted = peers - 1 + 3

    beside = sorted({(a % nyp, b % nzp) for a in (-1, 0, 1) for b in (-1, 0, 1)} - {(0, 0)})
    beyond = sorted({2 % nzp, -2 % nzp} - {0})

    def block(a, b):
        return plane(2 * lax.rem(yp + a, nyp) + qy, 2 * lax.rem(zp + b, nzp) + qz)

    for a, b in beside:
        greet(block(a, b))
    greeted += len(beside)

    def tell(step, devices):
        for device in devices:
            pl.semaphore_signal(told.at[step], inc=1, device_id=device, device_id_type=MESH)

    def hear(step, devices):
        if devices:
            pl.semaphore_wait(told.at[step], len(devices))

    rounds = (
        [block(a, b) for a, b in beside],
        [block(0, b) for b in beyond],
        [member(k) for k in range(1, 4)],
    )

    count = count_ref[0]
    bucket = bucket_ref[0]
    rows = lax.broadcasted_iota(jnp.int32, (VOX, 1), 0)
    row_mask = (rows < count).astype(F32)
    loads[0].wait()
    x_ref[0] = (crop_ref[...].astype(F32) * row_mask).astype(BF16)

    pl.semaphore_wait(barrier, greeted)
    pending = []

    def send_block(src, dst, send, recv, k):
        copy = pltpu.make_async_remote_copy(
            src_ref=src, dst_ref=dst, send_sem=send.at[k - 1], recv_sem=recv.at[k - 1],
            device_id=member(k), device_id_type=MESH,
        )
        copy.start()
        pending.append(copy.wait_send)

    for k in (3, 1, 2):
        send_block(x_ref.at[0], x_ref.at[k], x_send, x_recv, k)

    lane_block = lax.broadcasted_iota(jnp.int32, (OWN, 128), 1) >> 5
    mine = pl.ds(pl.multiple_of(OWN * fs, OWN), OWN)
    loads[1].wait()
    for g in range(TILES):
        tile = jnp.zeros((OWN, 128), F32)
        for j in range(4):
            if 4 * g + j < TAPS:
                tap = weight_ref[4 * g + j].astype(F32)
                tap = pltpu.roll(tap, lax.rem(32 * (j - q) + 128, 128), 1)
                tile = jnp.where(lane_block == j, tap, tile)
        wg_ref[mine, pl.ds(128 * g, 128)] = tile.astype(BF16)


    chips_x = peers // 2
    sibling = (dp, fs + 1 - 2 * lax.rem(fs, 2))

    def piece(k):
        return pl.ds(pl.multiple_of(OWN * lax.rem(fs + 2 * k, peers), OWN), OWN)

    def send_piece(rows, index, device):
        copy = pltpu.make_async_remote_copy(
            src_ref=wg_ref.at[rows, :], dst_ref=wg_ref.at[rows, :],
            send_sem=w_send.at[index], recv_sem=w_recv.at[index], device_id=device, device_id_type=MESH,
        )
        copy.start()
        pending.append(copy.wait_send)

    for k in range(1, chips_x):
        send_piece(mine, k - 1, along(2 * k))
    send_piece(mine, chips_x - 1, sibling)
    tell(0, rounds[0])
    for load in loads[2:]:
        load.wait()
    ct_ref[...] = cot_ref[...].astype(F32).T.astype(BF16)
    bias_rows = lax.broadcasted_iota(jnp.int32, (8, OUTS), 0)
    bias_row = jnp.sum(jnp.where(bias_rows == bucket, bias_ref[...], 0.0), axis=0, keepdims=True)
    meta_ref[0] = jnp.where(bias_rows == 0, bias_row, count.astype(F32))

    for k in range(1, 4):
        to = pl.ds(pl.multiple_of(QUARTER * (q ^ k), QUARTER), QUARTER)
        send_block(meta_ref.at[0], meta_ref.at[k], m_send, m_recv, k)
        send_block(ct_ref.at[to, :], c4_ref.at[k], c_send, c_recv, k)
    quarter = pl.ds(pl.multiple_of(QUARTER * q, QUARTER), QUARTER)
    c4_ref[0] = ct_ref[quarter, :]

    for k in range(1, 4):
        wait_bytes(meta_ref.at[k], m_recv.at[k - 1])
    table = jnp.concatenate(
        [meta_ref[k, 0:1, :] for k in range(4)]
        + [gain_ref[...], shift_ref[...], jnp.zeros((122, OUTS), F32)],
        axis=0,
    )
    par_ref[...] = table.T
    params = par_ref[quarter, :]
    param_lane = lax.broadcasted_iota(jnp.int32, (QUARTER, OUTS), 1)

    def column(index):
        return jnp.sum(jnp.where(param_lane == index, params, 0.0), axis=1, keepdims=True)

    gain = column(4)
    shift = column(5)

    for k in range(1, chips_x):
        source = piece(chips_x - k)
        wait_bytes(wg_ref.at[source, :], w_recv.at[k - 1])
        send_piece(source, chips_x - 1 + k, sibling)
    hear(0, rounds[0])
    tell(1, rounds[1])
    for k in range(chips_x):
        wait_bytes(wg_ref.at[mine, :], w_recv.at[chips_x - 1 + k])
    for g in range(TILES):
        wt_ref[pl.ds(128 * g, 128), :] = wg_ref[:, pl.ds(128 * g, 128)].astype(F32).T.astype(BF16)

    zf, yf, xf = lane_fields()
    reach = {
        (axis, offset): inside(offset, field, cells).astype(F32)
        for axis, field, cells in (("z", zf, 4), ("y", yf, 8), ("x", xf, 8))
        for offset in (-1, 1)
    }

    def moved(value, axis, offset, step):
        if offset == 0:
            return value
        rolled = pltpu.roll(value, (-offset * step) % VOX, 1)
        return rolled * reach[axis, offset]

    def group_sum(value):
        grouped = value.reshape(QUARTER // 8, 8, VOX)
        total = jnp.sum(jnp.sum(grouped, axis=2, keepdims=True), axis=1, keepdims=True)
        return total


    lane = lax.broadcasted_iota(jnp.int32, (1, VOX), 1).astype(F32)

    def spread(total):
        return jnp.broadcast_to(total, (QUARTER // 8, 8, VOX)).reshape(QUARTER, VOX)

    def normalize(m, pre):
        cells = meta_ref[m][1:2, 0:1]
        mask = (lane < cells).astype(F32)
        inverse = (1.0 / (cells * 8.0)).reshape(1, 1, 1)
        mean = spread(group_sum(pre * mask) * inverse)
        centered = pre - mean
        variance = group_sum(centered * centered * mask) * inverse
        scale = spread(lax.rsqrt(variance + EPSILON))
        normed = centered * scale
        value = normed * gain + shift + column(m)
        sig = 1.0 / (1.0 + jnp.exp(-value))
        acts_ref[m] = (value * sig * mask).astype(BF16)
        d_normed = c4_ref[m].astype(F32) * mask * (sig * (1.0 + value * (1.0 - sig))) * gain
        mean_d = spread(group_sum(d_normed) * inverse)
        mean_dn = spread(group_sum(d_normed * normed) * inverse)
        grad = scale * (d_normed - mask * (mean_d + normed * mean_dn))
        return grad.astype(BF16).astype(F32)

    def crops_of(pair):
        xts, pre, sum_z, sum_y, grads = {}, {}, {}, {}, {}
        for m in pair:
            if m > 0:
                wait_bytes(x_ref.at[m], x_recv.at[m - 1])
                wait_bytes(c4_ref.at[m], c_recv.at[m - 1])
        for m in pair:
            xts[m] = x_ref[m].astype(F32).T.astype(BF16)
            xt_ref[m] = xts[m]
            pre[m] = jnp.zeros((QUARTER, VOX), F32)
        for g in range(TILES):
            for m in pair:
                product = jnp.dot(wt_ref[pl.ds(128 * g, 128), :], xts[m], preferred_element_type=F32)
                for j in range(4):
                    t = 4 * g + j
                    if t >= TAPS:
                        continue
                    a, b, e = t // 9 - 1, t // 3 % 3 - 1, t % 3 - 1
                    part = moved(product[32 * j : 32 * j + 32], "x", e, 1)
                    sum_y[m] = part if e == -1 else sum_y[m] + part
                    if e == 1:
                        part = moved(sum_y[m], "y", b, 8)
                        sum_z[m] = part if b == -1 else sum_z[m] + part
                        if b == 1:
                            pre[m] = pre[m] + moved(sum_z[m], "z", a, 64)
        for m in pair:
            grads[m] = normalize(m, pre[m])
        for a in range(-1, 2):
            grad_a = {m: moved(grads[m], "z", -a, 64) for m in pair}
            for b in range(-1, 2):
                grad_ab = {m: moved(grad_a[m], "y", -b, 8) for m in pair}
                for e in range(-1, 2):
                    t = 9 * (a + 1) + 3 * (b + 1) + e + 1
                    for m in pair:
                        g_ref[m, pl.ds(32 * t, 32), :] = moved(grad_ab[m], "x", -e, 1).astype(BF16)
        for m in pair:
            g_ref[m, pl.ds(32 * TAPS, 32), :] = jnp.zeros((32, VOX), BF16)

    crops_of((0, 1))
    crops_of((2, 3))
    hear(1, rounds[1])
    tell(2, rounds[2])

    for k in range(1, 4):
        copy = pltpu.make_async_remote_copy(
            src_ref=acts_ref.at[k], dst_ref=actr_ref.at[quarter, :],
            send_sem=a_send.at[k - 1], recv_sem=a_recv.at[k - 1],
            device_id=member(k), device_id_type=MESH,
        )
        copy.start()
        pending.append(copy.wait_send)
    actr_ref[quarter, :] = acts_ref[0]

    side_c = lax.rem(fs, 2)
    chip_x = fs // 2
    for index, (start, width) in enumerate(CHUNKS):
        lanes = pl.ds(start, width)
        total = jnp.zeros((chans, width), F32)
        for m in range(4):
            total = total + lax.dot_general(
                xt_ref[m], g_ref[m, lanes, :], (((1,), (1,)), ((), ())), preferred_element_type=F32
            )
        dwf_ref[:, :, :, lanes] = total.reshape(chips_x, 2, OWN, width)
        copy = pltpu.make_async_remote_copy(
            src_ref=dwf_ref.at[:, 1 - side_c, :, lanes], dst_ref=d0r_ref.at[:, :, lanes],
            send_sem=d0_send.at[index], recv_sem=d0_recv.at[index], device_id=sibling, device_id_type=MESH,
        )
        copy.start()
        pending.append(copy.wait_send)
    for index, (start, width) in enumerate(CHUNKS):
        lanes = pl.ds(start, width)
        wait_bytes(d0r_ref.at[:, :, lanes], d0_recv.at[index])
        total = dwf_ref[:, side_c, :, lanes] + d0r_ref[:, :, lanes]
        d0r_ref[:, :, lanes] = total
        d1s_ref[:, :, lanes] = total.astype(BF16)
        for k in range(1, chips_x):
            copy = pltpu.make_async_remote_copy(
                src_ref=d1s_ref.at[lax.rem(chip_x + k, chips_x), :, lanes], dst_ref=d1r_ref.at[k - 1, :, lanes],
                send_sem=d1_send.at[index, k - 1], recv_sem=d1_recv.at[index],
                device_id=along(2 * k), device_id_type=MESH,
            )
            copy.start()
            pending.append(copy.wait_send)
    hear(2, rounds[2])

    spacing = nzp // spots

    def owner(u):
        return u // per_row, u % per_row // per_dev * spacing

    for index, (start, width) in enumerate(CHUNKS):
        lanes = pl.ds(start, width)
        if chips_x > 1:
            wait_bytes(d1r_ref.at[:, :, lanes], d1_recv.at[index])
        total = d0r_ref[chip_x, :, lanes]
        for k in range(1, chips_x):
            total = total + d1r_ref[k - 1, :, lanes].astype(F32)
        for g in range(start // 128, (start + width) // 128):
            for h in range(2):
                u = 2 * g + h
                at = 128 * g - start
                s_ref[u] = total[16 * h : 16 * h + 16, at : at + 128]
                oy, oz = owner(u)
                away = jnp.logical_or(yp != oy, zp != oz)
                slot = lax.rem(yp - oy + nyp, nyp) * nzp + lax.rem(zp - oz + nzp, nzp) - 1
                copy = pltpu.make_async_remote_copy(
                    src_ref=s_ref.at[u],
                    dst_ref=r2_ref.at[u % per_dev, jnp.maximum(slot, 0)],
                    send_sem=d2_send.at[u], recv_sem=d2_recv.at[u % per_dev],
                    device_id=plane(2 * oy + qy, 2 * oz + qz), device_id_type=MESH,
                )
                pl.when(away)(copy.start)
                pending.append(functools.partial(pl.when(away), copy.wait_send))

    owns = lax.rem(zp, spacing) == 0
    my_spot = zp // spacing
    first = yp * per_row + my_spot * per_dev
    owns = jnp.logical_and(owns, first < REAL)
    own_units = f_ref.at[pl.ds(first, per_dev), qy, qz]

    def unit_copy(k):
        return pltpu.make_async_remote_copy(
            src_ref=own_units, dst_ref=own_units,
            send_sem=e1_send.at[k - 1], recv_sem=e1_recv.at[my_spot, qz],
            device_id=plane(y, lax.rem(z + k, nz)), device_id_type=MESH,
        )

    @pl.when(owns)
    def _():
        for i in range(per_dev):
            u = first + i

            @pl.when(u < REAL)
            def _():
                wait_bytes(r2_ref.at[i], d2_recv.at[i])
                total = s_ref[u]
                for k in range(nyp * nzp - 1):
                    total = total + r2_ref[i, k]
                f_ref[u, qy, qz] = total.astype(BF16)

            @pl.when(u >= REAL)
            def _():
                f_ref[u, qy, qz] = jnp.zeros((16, 128), BF16)

        for k in sorted(range(1, nz), key=lambda k: min(k, nz - k)):
            unit_copy(k).start()

    def sent():
        @pl.when(owns)
        def _():
            for k in range(1, nz):
                unit_copy(k).wait_send()

    pending.append(sent)

    for k in range(1, 4):
        theirs = pl.ds(pl.multiple_of(QUARTER * (q ^ k), QUARTER), QUARTER)
        wait_bytes(actr_ref.at[theirs, :], a_recv.at[k - 1])
    act_ref[...] = actr_ref[...].astype(F32).T.astype(BF16)


    def start_of(row, spot):
        return (row // 2) * per_row + spot * per_dev

    def row_units(row, spot):
        return f_ref.at[pl.ds(start_of(row, spot), per_dev), lax.rem(row, 2)]

    def row_copy(spot, k):
        return pltpu.make_async_remote_copy(
            src_ref=row_units(y, spot), dst_ref=row_units(y, spot),
            send_sem=e2_send.at[spot, k - 1], recv_sem=e2_recv.at[spot, k - 1],
            device_id=plane(lax.rem(y + k, ny), z), device_id_type=MESH,
        )

    far_first = sorted(range(1, ny), key=lambda k: -min(k, ny - k))

    def pass_on(spot):
        at = spot * spacing

        @pl.when(start_of(y, spot) < REAL)
        def _():
            for side in range(2):
                @pl.when(jnp.logical_not(jnp.logical_and(zp == at, qz == side)))
                def _():
                    units = f_ref.at[pl.ds(start_of(y, spot), per_dev), qy, side]
                    wait_bytes(units, e1_recv.at[spot, side])

            for k in far_first:
                row_copy(spot, k).start()

    def row_sent():
        for spot in range(spots):
            @pl.when(start_of(y, spot) < REAL)
            def _():
                for k in range(1, ny):
                    row_copy(spot, k).wait_send()

    pending.append(row_sent)
    nearest = (zp + spacing // 2) // spacing
    for step in (0, 1, spots - 1, 2)[:spots]:
        pass_on(lax.rem(nearest + step, spots))
    for k in range(1, ny):
        from_row = lax.rem(y + ny - k, ny)
        for spot in range(spots):
            @pl.when(start_of(from_row, spot) < REAL)
            def _():
                wait_bytes(row_units(from_row, spot), e2_recv.at[spot, k - 1])


    block16 = lax.broadcasted_iota(jnp.int32, (16, 128), 1) >> 5
    for g in range(TILES):
        for h in range(2):
            quarters = [f_ref[2 * g + h, p // 2, p % 2].astype(F32) for p in range(4)]
            for j in range(4):
                t = 4 * g + j
                if t >= TAPS:
                    continue
                line = jnp.zeros((16, 128), F32)
                for p in range(4):
                    turned = quarters[p] if p == j else pltpu.roll(quarters[p], (32 * (p - j)) % 128, 1)
                    line = jnp.where(block16 == p, turned, line)
                grad_ref[t, 16 * h : 16 * h + 16, :] = line
    for wait in pending:
        wait()

def body(geometry, crops, weight, bucket_bias, norm_gain, norm_shift, bucket_ids, valid_counts, cotangent):
    ny, nz, peers = geometry
    nyp, nzp = ny // 2, nz // 2
    per_row = UNITS // nyp
    spots = min(per_row, nzp, 4)
    per_dev = per_row // spots
    chans = OWN * peers
    others = max(1, peers - 1)
    smem = pl.BlockSpec(memory_space=pltpu.SMEM)
    vmem = pl.BlockSpec(memory_space=pltpu.VMEM)
    dma = pltpu.SemaphoreType.DMA
    def hold(x):
        return pltpu.with_memory_space_constraint(x, pltpu.HBM)

    activated, grad = pl.pallas_call(
        functools.partial(kernel, geometry),
        out_shape=(
            jax.ShapeDtypeStruct((VOX, OUTS), BF16),
            jax.ShapeDtypeStruct((TAPS, OWN, OUTS), F32),
        ),
        in_specs=[smem, smem] + [pl.BlockSpec(memory_space=pltpu.HBM)] * 6,
        out_specs=(vmem, vmem),
        scratch_shapes=[
            pltpu.VMEM((VOX, chans), BF16),
            pltpu.VMEM((TAPS, OWN, OUTS), BF16),
            pltpu.VMEM(bucket_bias.shape, F32),
            pltpu.VMEM((1, OUTS), F32),
            pltpu.VMEM((1, OUTS), F32),
            pltpu.VMEM((VOX, OUTS), BF16),
            dma((6,)),
            pltpu.VMEM((4, VOX, chans), BF16),
            pltpu.VMEM((4, chans, VOX), BF16),
            pltpu.VMEM((chans, COLS), BF16),
            pltpu.VMEM((COLS, chans), BF16),
            pltpu.VMEM((OUTS, VOX), BF16),
            pltpu.VMEM((4, QUARTER, VOX), BF16),
            pltpu.VMEM((4, 8, OUTS), F32),
            pltpu.VMEM((OUTS, OUTS), F32),
            pltpu.VMEM((4, COLS, VOX), BF16),
            pltpu.VMEM((peers // 2, 2, OWN, COLS), F32),
            pltpu.VMEM((peers // 2, OWN, COLS), F32),
            pltpu.VMEM((peers // 2, OWN, COLS), BF16),
            pltpu.VMEM((max(1, peers // 2 - 1), OWN, COLS), BF16),
            pltpu.VMEM((REAL, 16, 128), F32),
            pltpu.VMEM((per_dev, max(1, nyp * nzp - 1), 16, 128), F32),
            pltpu.VMEM((UNITS, 2, 2, 16, 128), BF16),
            pltpu.VMEM((4, QUARTER, VOX), BF16),
            pltpu.VMEM((OUTS, VOX), BF16),
            pltpu.SemaphoreType.REGULAR((3,)),
            dma((others,)), dma((others,)),
            dma((3,)), dma((3,)),
            dma((3,)), dma((3,)),
            dma((3,)), dma((3,)),
            dma((3,)), dma((3,)),
            dma((len(CHUNKS),)), dma((len(CHUNKS),)),
            dma((len(CHUNKS), others)), dma((len(CHUNKS),)),
            dma((REAL,)), dma((per_dev,)),
            dma((nz - 1,)), dma((spots, 2)),
            dma((spots, ny - 1)), dma((spots, ny - 1)),
        ],
        compiler_params=pltpu.CompilerParams(
            collective_id=0, has_side_effects=True, vmem_limit_bytes=40 * 1024 * 1024
        ),
    )(
        valid_counts, bucket_ids,
        hold(crops.reshape(VOX, chans)), hold(weight.transpose(1, 0, 2)), hold(bucket_bias),
        hold(norm_gain.reshape(1, OUTS)), hold(norm_shift.reshape(1, OUTS)), hold(cotangent.reshape(VOX, OUTS)),
    )
    return activated[None], grad.transpose(1, 0, 2)


def solution(mesh):
    chips = mesh.shape["dp"]
    ny = 8 if chips == 128 else 2
    geometry = (ny, chips // ny, mesh.shape["fsdp"])
    return jax.shard_map(
        functools.partial(body, geometry),
        mesh=mesh,
        in_specs=(
            P(("dp", "fsdp"), None, None, None, None),
            P("fsdp", None, None),
            P(),
            P(),
            P(),
            P(("dp", "fsdp")),
            P(("dp", "fsdp")),
            P(("dp", "fsdp"), None, None),
        ),
        out_specs=(P(("dp", "fsdp"), None, None), P("fsdp", None, None)),
        check_vma=False,
    )
```

```python
import functools

import jax
import jax.numpy as jnp
from jax import lax
from jax.experimental import pallas as pl
from jax.experimental.pallas import tpu as pltpu
from jax.sharding import PartitionSpec as P

MESH = pl.DeviceIdType.MESH
F32 = jnp.float32
BF16 = jnp.bfloat16

EPSILON = 1e-05
VOX = 256
OWN = 32
OUTS = 128
QUARTER = 32
TAPS = 27
TILES = 7
COLS = TILES * 128
UNITS = 16
REAL = 2 * TILES
CHUNKS = ((0, 256), (256, 256), (512, 256), (768, 128))


def lane_fields():
    lane = lax.broadcasted_iota(jnp.int32, (8, VOX), 1)
    return lane >> 6, (lane >> 3) & 7, lane & 7


def inside(offset, field, cells):
    moved = field + offset
    return jnp.logical_and(moved >= 0, moved < cells)[0:1]


def wait_bytes(ref, sem):
    pltpu.make_async_copy(ref, ref, sem).wait()


def kernel(
    geometry,
    count_ref, bucket_ref, crop_hbm, weight_hbm, bias_hbm, gain_hbm, shift_hbm, cot_hbm,
    act_ref, grad_ref,
    crop_ref, weight_ref, bias_ref, gain_ref, shift_ref, cot_ref, in_sem,
    x_ref, xt_ref, wg_ref, wt_ref, ct_ref, c4_ref, meta_ref, par_ref,
    g_ref, dwf_ref, d0r_ref, d1s_ref, d1r_ref, s_ref, r2_ref, f_ref, acts_ref, actr_ref,
    told, w_send, w_recv, x_send, x_recv, c_send, c_recv, m_send, m_recv, a_send, a_recv,
    d0_send, d0_recv, d1_send, d1_recv, d2_send, d2_recv, e1_send, e1_recv, e2_send, e2_recv,
):
    ny, nz, peers = geometry
    nyp, nzp = ny // 2, nz // 2
    per_row = UNITS // nyp
    spots = min(per_row, nzp, 4)
    per_dev = per_row // spots
    chans = OWN * peers

    dp = lax.axis_index("dp")
    fs = lax.axis_index("fsdp")
    y, z = dp // nz, dp % nz
    yp, zp, qy, qz = y // 2, z // 2, y % 2, z % 2
    q = qy * 2 + qz

    def plane(yy, zz):
        return (yy * nz + zz, fs)

    def along(k):
        return (dp, lax.rem(fs + k, peers))

    def member(k):
        return plane(2 * yp + (qy ^ (k >> 1)), 2 * zp + (qz ^ (k & 1)))

    loads = [
        pltpu.make_async_copy(src, dst, in_sem.at[index])
        for index, (src, dst) in enumerate((
            (crop_hbm, crop_ref), (weight_hbm, weight_ref), (cot_hbm, cot_ref),
            (bias_hbm, bias_ref), (gain_hbm, gain_ref), (shift_hbm, shift_ref),
        ))
    ]
    for load in loads:
        load.start()

    barrier = pltpu.get_barrier_semaphore()

    def greet(device):
        pl.semaphore_signal(barrier, inc=1, device_id=device, device_id_type=MESH)

    for k in range(1, peers):
        greet(along(k))
    for k in range(1, 4):
        greet(member(k))
    greeted = peers - 1 + 3

    def offsets(*pairs):
        return sorted({(a % nyp, b % nzp) for a, b in pairs} - {(0, 0)})

    beside = offsets((0, 1), (0, -1), (1, 0), (-1, 0))
    second = offsets((0, 2), (0, -2), (2, 0), (1, 1), (1, -1), (-1, 1), (-1, -1))
    along_z = offsets((0, 2), (0, -2))

    def block(a, b):
        return plane(2 * lax.rem(yp + a, nyp) + qy, 2 * lax.rem(zp + b, nzp) + qz)

    for a, b in beside:
        greet(block(a, b))
    greeted += len(beside)

    def tell(step, devices):
        for device in devices:
            pl.semaphore_signal(told.at[step], inc=1, device_id=device, device_id_type=MESH)

    def hear(step, devices):
        if devices:
            pl.semaphore_wait(told.at[step], len(devices))

    rounds = (
        [block(a, b) for a, b in beside],
        [block(a, b) for a, b in second],
        [block(a, b) for a, b in along_z],
        [member(k) for k in range(1, 4)],
    )

    count = count_ref[0]
    bucket = bucket_ref[0]
    rows = lax.broadcasted_iota(jnp.int32, (VOX, 1), 0)
    row_mask = (rows < count).astype(F32)
    loads[0].wait()
    x_ref[0] = (crop_ref[...].astype(F32) * row_mask).astype(BF16)

    lane_block = lax.broadcasted_iota(jnp.int32, (OWN, 128), 1) >> 5
    mine = pl.ds(pl.multiple_of(OWN * fs, OWN), OWN)
    loads[1].wait()
    for g in range(TILES):
        tile = jnp.zeros((OWN, 128), F32)
        for j in range(4):
            if 4 * g + j < TAPS:
                tap = weight_ref[4 * g + j].astype(F32)
                tap = pltpu.roll(tap, lax.rem(32 * (j - q) + 128, 128), 1)
                tile = jnp.where(lane_block == j, tap, tile)
        wg_ref[mine, pl.ds(128 * g, 128)] = tile.astype(BF16)

    for load in loads[2:]:
        load.wait()
    ct_ref[...] = cot_ref[...].astype(F32).T.astype(BF16)
    bias_rows = lax.broadcasted_iota(jnp.int32, (8, OUTS), 0)
    bias_row = jnp.sum(jnp.where(bias_rows == bucket, bias_ref[...], 0.0), axis=0, keepdims=True)
    meta_ref[0] = jnp.where(bias_rows == 0, bias_row, count.astype(F32))

    pl.semaphore_wait(barrier, greeted)
    pending = []

    def send_block(src, dst, send, recv, k):
        copy = pltpu.make_async_remote_copy(
            src_ref=src, dst_ref=dst, send_sem=send.at[k - 1], recv_sem=recv.at[k - 1],
            device_id=member(k), device_id_type=MESH,
        )
        copy.start()
        pending.append(copy.wait_send)

    chips_x = peers // 2
    sibling = (dp, fs + 1 - 2 * lax.rem(fs, 2))

    def piece(k):
        return pl.ds(pl.multiple_of(OWN * lax.rem(fs + 2 * k, peers), OWN), OWN)

    def send_piece(rows, index, device):
        copy = pltpu.make_async_remote_copy(
            src_ref=wg_ref.at[rows, :], dst_ref=wg_ref.at[rows, :],
            send_sem=w_send.at[index], recv_sem=w_recv.at[index], device_id=device, device_id_type=MESH,
        )
        copy.start()
        pending.append(copy.wait_send)

    for k in range(1, chips_x):
        send_piece(mine, k - 1, along(2 * k))
    send_piece(mine, chips_x - 1, sibling)
    for k in range(1, 4):
        send_block(meta_ref.at[0], meta_ref.at[k], m_send, m_recv, k)
    for k in (3, 1, 2):
        send_block(x_ref.at[0], x_ref.at[k], x_send, x_recv, k)

    for k in range(1, 4):
        to = pl.ds(pl.multiple_of(QUARTER * (q ^ k), QUARTER), QUARTER)
        send_block(ct_ref.at[to, :], c4_ref.at[k], c_send, c_recv, k)
    tell(0, rounds[0])
    quarter = pl.ds(pl.multiple_of(QUARTER * q, QUARTER), QUARTER)
    c4_ref[0] = ct_ref[quarter, :]

    for k in range(1, 4):
        wait_bytes(meta_ref.at[k], m_recv.at[k - 1])
    table = jnp.concatenate(
        [meta_ref[k, 0:1, :] for k in range(4)]
        + [gain_ref[...], shift_ref[...], jnp.zeros((122, OUTS), F32)],
        axis=0,
    )
    par_ref[...] = table.T
    hear(0, rounds[0])
    tell(1, rounds[1])
    params = par_ref[quarter, :]
    param_lane = lax.broadcasted_iota(jnp.int32, (QUARTER, OUTS), 1)

    def column(index):
        return jnp.sum(jnp.where(param_lane == index, params, 0.0), axis=1, keepdims=True)

    gain = column(4)
    shift = column(5)

    for k in range(1, chips_x):
        source = piece(chips_x - k)
        wait_bytes(wg_ref.at[source, :], w_recv.at[k - 1])
        send_piece(source, chips_x - 1 + k, sibling)
    for k in range(chips_x):
        wait_bytes(wg_ref.at[mine, :], w_recv.at[chips_x - 1 + k])
    for g in range(TILES):
        wt_ref[pl.ds(128 * g, 128), :] = wg_ref[:, pl.ds(128 * g, 128)].astype(F32).T.astype(BF16)

    zf, yf, xf = lane_fields()
    reach = {
        (axis, offset): inside(offset, field, cells).astype(F32)
        for axis, field, cells in (("z", zf, 4), ("y", yf, 8), ("x", xf, 8))
        for offset in (-1, 1)
    }

    def moved(value, axis, offset, step):
        if offset == 0:
            return value
        rolled = pltpu.roll(value, (-offset * step) % VOX, 1)
        return rolled * reach[axis, offset]

    def group_sum(value):
        grouped = value.reshape(QUARTER // 8, 8, VOX)
        total = jnp.sum(jnp.sum(grouped, axis=2, keepdims=True), axis=1, keepdims=True)
        return total


    lane = lax.broadcasted_iota(jnp.int32, (1, VOX), 1).astype(F32)

    def spread(total):
        return jnp.broadcast_to(total, (QUARTER // 8, 8, VOX)).reshape(QUARTER, VOX)

    def normalize(m, pre):
        cells = meta_ref[m][1:2, 0:1]
        mask = (lane < cells).astype(F32)
        inverse = (1.0 / (cells * 8.0)).reshape(1, 1, 1)
        mean = spread(group_sum(pre * mask) * inverse)
        centered = pre - mean
        variance = group_sum(centered * centered * mask) * inverse
        scale = spread(lax.rsqrt(variance + EPSILON))
        normed = centered * scale
        value = normed * gain + shift + column(m)
        sig = 1.0 / (1.0 + jnp.exp(-value))
        acts_ref[m] = (value * sig * mask).astype(BF16)
        d_normed = c4_ref[m].astype(F32) * mask * (sig * (1.0 + value * (1.0 - sig))) * gain
        mean_d = spread(group_sum(d_normed) * inverse)
        mean_dn = spread(group_sum(d_normed * normed) * inverse)
        grad = scale * (d_normed - mask * (mean_d + normed * mean_dn))
        return grad.astype(BF16).astype(F32)

    def crops_of(pair, between=None):
        xts, pre, sum_z, sum_y, grads = {}, {}, {}, {}, {}
        for m in pair:
            if m > 0:
                wait_bytes(x_ref.at[m], x_recv.at[m - 1])
        for m in pair:
            xts[m] = x_ref[m].astype(F32).T.astype(BF16)
            xt_ref[m] = xts[m]
            pre[m] = jnp.zeros((QUARTER, VOX), F32)
        for g in range(TILES):
            for m in pair:
                product = jnp.dot(wt_ref[pl.ds(128 * g, 128), :], xts[m], preferred_element_type=F32)
                for j in range(4):
                    t = 4 * g + j
                    if t >= TAPS:
                        continue
                    a, b, e = t // 9 - 1, t // 3 % 3 - 1, t % 3 - 1
                    part = moved(product[32 * j : 32 * j + 32], "x", e, 1)
                    sum_y[m] = part if e == -1 else sum_y[m] + part
                    if e == 1:
                        part = moved(sum_y[m], "y", b, 8)
                        sum_z[m] = part if b == -1 else sum_z[m] + part
                        if b == 1:
                            pre[m] = pre[m] + moved(sum_z[m], "z", a, 64)
        if between is not None:
            between()
        for m in pair:
            if m > 0:
                wait_bytes(c4_ref.at[m], c_recv.at[m - 1])
        for m in pair:
            grads[m] = normalize(m, pre[m])
        for a in range(-1, 2):
            grad_a = {m: moved(grads[m], "z", -a, 64) for m in pair}
            for b in range(-1, 2):
                grad_ab = {m: moved(grad_a[m], "y", -b, 8) for m in pair}
                for e in range(-1, 2):
                    t = 9 * (a + 1) + 3 * (b + 1) + e + 1
                    for m in pair:
                        g_ref[m, pl.ds(32 * t, 32), :] = moved(grad_ab[m], "x", -e, 1).astype(BF16)
        for m in pair:
            g_ref[m, pl.ds(32 * TAPS, 32), :] = jnp.zeros((32, VOX), BF16)

    def gradient(pair, lanes, width):
        total = None
        for m in pair:
            term = lax.dot_general(
                xt_ref[m], g_ref[m, lanes, :], (((1,), (1,)), ((), ())), preferred_element_type=F32
            )
            total = term if total is None else total + term
        return total.reshape(chips_x, 2, OWN, width)

    def second_round():
        hear(1, rounds[1])
        tell(2, rounds[2])

    crops_of((0, 1), second_round)
    for start, width in CHUNKS:
        lanes = pl.ds(start, width)
        dwf_ref[:, :, :, lanes] = gradient((0, 1), lanes, width)
    crops_of((2, 3))
    for k in range(1, 4):
        copy = pltpu.make_async_remote_copy(
            src_ref=acts_ref.at[k], dst_ref=actr_ref.at[quarter, :],
            send_sem=a_send.at[k - 1], recv_sem=a_recv.at[k - 1],
            device_id=member(k), device_id_type=MESH,
        )
        copy.start()
        pending.append(copy.wait_send)
    actr_ref[quarter, :] = acts_ref[0]

    side_c = lax.rem(fs, 2)
    chip_x = fs // 2
    for index, (start, width) in enumerate(CHUNKS):
        lanes = pl.ds(start, width)
        dwf_ref[:, :, :, lanes] += gradient((2, 3), lanes, width)
        copy = pltpu.make_async_remote_copy(
            src_ref=dwf_ref.at[:, 1 - side_c, :, lanes], dst_ref=d0r_ref.at[:, :, lanes],
            send_sem=d0_send.at[index], recv_sem=d0_recv.at[index], device_id=sibling, device_id_type=MESH,
        )
        copy.start()
        pending.append(copy.wait_send)
    hear(2, rounds[2])
    tell(3, rounds[3])
    for index, (start, width) in enumerate(CHUNKS):
        lanes = pl.ds(start, width)
        wait_bytes(d0r_ref.at[:, :, lanes], d0_recv.at[index])
        total = dwf_ref[:, side_c, :, lanes] + d0r_ref[:, :, lanes]
        d0r_ref[:, :, lanes] = total
        d1s_ref[:, :, lanes] = total.astype(BF16)
        for k in sorted(range(1, chips_x), key=lambda k: -min(k, chips_x - k)):
            copy = pltpu.make_async_remote_copy(
                src_ref=d1s_ref.at[lax.rem(chip_x + k, chips_x), :, lanes], dst_ref=d1r_ref.at[k - 1, :, lanes],
                send_sem=d1_send.at[index, k - 1], recv_sem=d1_recv.at[index],
                device_id=along(2 * k), device_id_type=MESH,
            )
            copy.start()
            pending.append(copy.wait_send)
    hear(3, rounds[3])

    spacing = nzp // spots

    def owner(u):
        return u // per_row, u % per_row // per_dev * spacing + spacing - 1

    for index, (start, width) in enumerate(CHUNKS):
        lanes = pl.ds(start, width)
        if chips_x > 1:
            wait_bytes(d1r_ref.at[:, :, lanes], d1_recv.at[index])
        total = d0r_ref[chip_x, :, lanes]
        for k in range(1, chips_x):
            total = total + d1r_ref[k - 1, :, lanes].astype(F32)
        for g in range(start // 128, (start + width) // 128):
            for h in range(2):
                u = 2 * g + h
                at = 128 * g - start
                s_ref[u] = total[16 * h : 16 * h + 16, at : at + 128]
                oy, oz = owner(u)
                away = jnp.logical_or(yp != oy, zp != oz)
                slot = lax.rem(yp - oy + nyp, nyp) * nzp + lax.rem(zp - oz + nzp, nzp) - 1
                copy = pltpu.make_async_remote_copy(
                    src_ref=s_ref.at[u],
                    dst_ref=r2_ref.at[u % per_dev, jnp.maximum(slot, 0)],
                    send_sem=d2_send.at[u], recv_sem=d2_recv.at[u % per_dev],
                    device_id=plane(2 * oy + qy, 2 * oz + qz), device_id_type=MESH,
                )
                pl.when(away)(copy.start)
                pending.append(functools.partial(pl.when(away), copy.wait_send))

    owns = lax.rem(zp, spacing) == spacing - 1
    my_spot = zp // spacing
    first = yp * per_row + my_spot * per_dev
    owns = jnp.logical_and(owns, first < REAL)
    own_units = f_ref.at[pl.ds(first, per_dev), qy, qz]

    def unit_copy(target):
        return pltpu.make_async_remote_copy(
            src_ref=own_units, dst_ref=own_units,
            send_sem=e1_send.at[target], recv_sem=e1_recv.at[my_spot, qz],
            device_id=plane(y, target), device_id_type=MESH,
        )

    @pl.when(owns)
    def _():
        for i in range(per_dev):
            u = first + i

            @pl.when(u < REAL)
            def _():
                wait_bytes(r2_ref.at[i], d2_recv.at[i])
                total = s_ref[u]
                for k in range(nyp * nzp - 1):
                    total = total + r2_ref[i, k]
                f_ref[u, qy, qz] = total.astype(BF16)

            @pl.when(u >= REAL)
            def _():
                f_ref[u, qy, qz] = jnp.zeros((16, 128), BF16)

        for target in range(nz):
            pl.when(z != target)(unit_copy(target).start)

    def sent():
        @pl.when(owns)
        def _():
            for target in range(nz):
                pl.when(z != target)(unit_copy(target).wait_send)

    pending.append(sent)

    for k in range(1, 4):
        theirs = pl.ds(pl.multiple_of(QUARTER * (q ^ k), QUARTER), QUARTER)
        wait_bytes(actr_ref.at[theirs, :], a_recv.at[k - 1])
    act_ref[...] = actr_ref[...].astype(F32).T.astype(BF16)


    def start_of(row, spot):
        return (row // 2) * per_row + spot * per_dev

    def row_units(row, spot):
        return f_ref.at[pl.ds(start_of(row, spot), per_dev), lax.rem(row, 2)]

    def row_copy(spot, k):
        return pltpu.make_async_remote_copy(
            src_ref=row_units(y, spot), dst_ref=row_units(y, spot),
            send_sem=e2_send.at[spot, k - 1], recv_sem=e2_recv.at[spot, k - 1],
            device_id=plane(lax.rem(y + k, ny), z), device_id_type=MESH,
        )

    far_first = sorted(range(1, ny), key=lambda k: -min(k, ny - k))

    def pass_on(spot):
        at = spot * spacing + spacing - 1

        @pl.when(start_of(y, spot) < REAL)
        def _():
            for side in range(2):
                @pl.when(jnp.logical_not(jnp.logical_and(zp == at, qz == side)))
                def _():
                    units = f_ref.at[pl.ds(start_of(y, spot), per_dev), qy, side]
                    wait_bytes(units, e1_recv.at[spot, side])

            for k in far_first:
                row_copy(spot, k).start()

    def row_sent():
        for spot in range(spots):
            @pl.when(start_of(y, spot) < REAL)
            def _():
                for k in range(1, ny):
                    row_copy(spot, k).wait_send()

    pending.append(row_sent)
    nearest = zp // spacing
    for step in {4: (0, 3, 1, 2), 2: (0, 1), 1: (0,)}[spots]:
        pass_on(lax.rem(nearest + step, spots))
    for k in range(1, ny):
        from_row = lax.rem(y + ny - k, ny)
        for spot in range(spots):
            @pl.when(start_of(from_row, spot) < REAL)
            def _():
                wait_bytes(row_units(from_row, spot), e2_recv.at[spot, k - 1])


    block16 = lax.broadcasted_iota(jnp.int32, (16, 128), 1) >> 5
    for g in range(TILES):
        for h in range(2):
            quarters = [f_ref[2 * g + h, p // 2, p % 2].astype(F32) for p in range(4)]
            for j in range(4):
                t = 4 * g + j
                if t >= TAPS:
                    continue
                line = jnp.zeros((16, 128), F32)
                for p in range(4):
                    turned = quarters[p] if p == j else pltpu.roll(quarters[p], (32 * (p - j)) % 128, 1)
                    line = jnp.where(block16 == p, turned, line)
                grad_ref[t, 16 * h : 16 * h + 16, :] = line
    for wait in pending:
        wait()

def body(geometry, crops, weight, bucket_bias, norm_gain, norm_shift, bucket_ids, valid_counts, cotangent):
    ny, nz, peers = geometry
    nyp, nzp = ny // 2, nz // 2
    per_row = UNITS // nyp
    spots = min(per_row, nzp, 4)
    per_dev = per_row // spots
    chans = OWN * peers
    others = max(1, peers - 1)
    smem = pl.BlockSpec(memory_space=pltpu.SMEM)
    vmem = pl.BlockSpec(memory_space=pltpu.VMEM)
    dma = pltpu.SemaphoreType.DMA
    def hold(x):
        return pltpu.with_memory_space_constraint(x, pltpu.HBM)

    activated, grad = pl.pallas_call(
        functools.partial(kernel, geometry),
        out_shape=(
            jax.ShapeDtypeStruct((VOX, OUTS), BF16),
            jax.ShapeDtypeStruct((TAPS, OWN, OUTS), F32),
        ),
        in_specs=[smem, smem] + [pl.BlockSpec(memory_space=pltpu.HBM)] * 6,
        out_specs=(vmem, vmem),
        scratch_shapes=[
            pltpu.VMEM((VOX, chans), BF16),
            pltpu.VMEM((TAPS, OWN, OUTS), BF16),
            pltpu.VMEM(bucket_bias.shape, F32),
            pltpu.VMEM((1, OUTS), F32),
            pltpu.VMEM((1, OUTS), F32),
            pltpu.VMEM((VOX, OUTS), BF16),
            dma((6,)),
            pltpu.VMEM((4, VOX, chans), BF16),
            pltpu.VMEM((4, chans, VOX), BF16),
            pltpu.VMEM((chans, COLS), BF16),
            pltpu.VMEM((COLS, chans), BF16),
            pltpu.VMEM((OUTS, VOX), BF16),
            pltpu.VMEM((4, QUARTER, VOX), BF16),
            pltpu.VMEM((4, 8, OUTS), F32),
            pltpu.VMEM((OUTS, OUTS), F32),
            pltpu.VMEM((4, COLS, VOX), BF16),
            pltpu.VMEM((peers // 2, 2, OWN, COLS), F32),
            pltpu.VMEM((peers // 2, OWN, COLS), F32),
            pltpu.VMEM((peers // 2, OWN, COLS), BF16),
            pltpu.VMEM((max(1, peers // 2 - 1), OWN, COLS), BF16),
            pltpu.VMEM((REAL, 16, 128), F32),
            pltpu.VMEM((per_dev, max(1, nyp * nzp - 1), 16, 128), F32),
            pltpu.VMEM((UNITS, 2, 2, 16, 128), BF16),
            pltpu.VMEM((4, QUARTER, VOX), BF16),
            pltpu.VMEM((OUTS, VOX), BF16),
            pltpu.SemaphoreType.REGULAR((4,)),
            dma((others,)), dma((others,)),
            dma((3,)), dma((3,)),
            dma((3,)), dma((3,)),
            dma((3,)), dma((3,)),
            dma((3,)), dma((3,)),
            dma((len(CHUNKS),)), dma((len(CHUNKS),)),
            dma((len(CHUNKS), others)), dma((len(CHUNKS),)),
            dma((REAL,)), dma((per_dev,)),
            dma((nz,)), dma((spots, 2)),
            dma((spots, ny - 1)), dma((spots, ny - 1)),
        ],
        compiler_params=pltpu.CompilerParams(
            collective_id=0, has_side_effects=True, vmem_limit_bytes=40 * 1024 * 1024
        ),
    )(
        valid_counts, bucket_ids,
        hold(crops.reshape(VOX, chans)), hold(weight.transpose(1, 0, 2)), hold(bucket_bias),
        hold(norm_gain.reshape(1, OUTS)), hold(norm_shift.reshape(1, OUTS)), hold(cotangent.reshape(VOX, OUTS)),
    )
    return activated[None], grad.transpose(1, 0, 2)


def solution(mesh):
    chips = mesh.shape["dp"]
    ny = 8 if chips == 128 else 2
    geometry = (ny, chips // ny, mesh.shape["fsdp"])
    return jax.shard_map(
        functools.partial(body, geometry),
        mesh=mesh,
        in_specs=(
            P(("dp", "fsdp"), None, None, None, None),
            P("fsdp", None, None),
            P(),
            P(),
            P(),
            P(("dp", "fsdp")),
            P(("dp", "fsdp")),
            P(("dp", "fsdp"), None, None),
        ),
        out_specs=(P(("dp", "fsdp"), None, None), P("fsdp", None, None)),
        check_vma=False,
    )
```

```python
import functools

import jax
import jax.numpy as jnp
from jax import lax
from jax.experimental import pallas as pl
from jax.experimental.pallas import tpu as pltpu
from jax.sharding import PartitionSpec as P

MESH = pl.DeviceIdType.MESH
F32 = jnp.float32
BF16 = jnp.bfloat16

EPSILON = 1e-05
VOX = 256
OWN = 32
OUTS = 128
QUARTER = 32
TAPS = 27
TILES = 7
COLS = TILES * 128
UNITS = 16
REAL = 2 * TILES
SPOTS = {8: (7, 0, 1, 5)}
CHUNKS = ((0, 256), (256, 256), (512, 256), (768, 128))


def lane_fields():
    lane = lax.broadcasted_iota(jnp.int32, (8, VOX), 1)
    return lane >> 6, (lane >> 3) & 7, lane & 7


def inside(offset, field, cells):
    moved = field + offset
    return jnp.logical_and(moved >= 0, moved < cells)[0:1]


def wait_bytes(ref, sem):
    pltpu.make_async_copy(ref, ref, sem).wait()


def kernel(
    geometry,
    count_ref, bucket_ref, crop_hbm, weight_hbm, bias_hbm, gain_hbm, shift_hbm, cot_hbm,
    act_ref, grad_ref,
    crop_ref, weight_ref, bias_ref, gain_ref, shift_ref, cot_ref, in_sem,
    x_ref, xt_ref, wg_ref, wt_ref, ct_ref, c4_ref, meta_ref, par_ref,
    g_ref, dwf_ref, d0r_ref, d1s_ref, d1r_ref, s_ref, r2_ref, f_ref, acts_ref, actr_ref,
    told, w_send, w_recv, x_send, x_recv, c_send, c_recv, m_send, m_recv, a_send, a_recv,
    d0_send, d0_recv, d1_send, d1_recv, d2_send, d2_recv, e1_send, e1_recv, e2_send, e2_recv,
):
    ny, nz, peers = geometry
    nyp, nzp = ny // 2, nz // 2
    per_row = UNITS // nyp
    places = SPOTS.get(nzp, tuple(range(min(per_row, nzp, 4))))
    spots = len(places)
    per_dev = per_row // spots
    chans = OWN * peers

    dp = lax.axis_index("dp")
    fs = lax.axis_index("fsdp")
    y, z = dp // nz, dp % nz
    yp, zp, qy, qz = y // 2, z // 2, y % 2, z % 2
    q = qy * 2 + qz

    def plane(yy, zz):
        return (yy * nz + zz, fs)

    def along(k):
        return (dp, lax.rem(fs + k, peers))

    def member(k):
        return plane(2 * yp + (qy ^ (k >> 1)), 2 * zp + (qz ^ (k & 1)))

    loads = [
        pltpu.make_async_copy(src, dst, in_sem.at[index])
        for index, (src, dst) in enumerate((
            (crop_hbm, crop_ref), (weight_hbm, weight_ref), (cot_hbm, cot_ref),
            (bias_hbm, bias_ref), (gain_hbm, gain_ref), (shift_hbm, shift_ref),
        ))
    ]
    for load in loads:
        load.start()

    barrier = pltpu.get_barrier_semaphore()

    def greet(device):
        pl.semaphore_signal(barrier, inc=1, device_id=device, device_id_type=MESH)

    for k in range(1, peers):
        greet(along(k))
    for k in range(1, 4):
        greet(member(k))
    greeted = peers - 1 + 3

    def offsets(*pairs):
        return sorted({(a % nyp, b % nzp) for a, b in pairs} - {(0, 0)})

    beside = offsets((0, 1), (0, -1), (1, 0), (-1, 0))
    second = offsets((0, 2), (0, -2), (2, 0), (1, 1), (1, -1), (-1, 1), (-1, -1))
    along_z = offsets((0, 2), (0, -2))

    def block(a, b):
        return plane(2 * lax.rem(yp + a, nyp) + qy, 2 * lax.rem(zp + b, nzp) + qz)

    for a, b in beside:
        greet(block(a, b))
    greeted += len(beside)

    def tell(step, devices):
        for device in devices:
            pl.semaphore_signal(told.at[step], inc=1, device_id=device, device_id_type=MESH)

    def hear(step, devices):
        if devices:
            pl.semaphore_wait(told.at[step], len(devices))

    rounds = (
        [block(a, b) for a, b in beside],
        [block(a, b) for a, b in second],
        [block(a, b) for a, b in along_z],
        [member(k) for k in range(1, 4)],
    )

    count = count_ref[0]
    bucket = bucket_ref[0]
    rows = lax.broadcasted_iota(jnp.int32, (VOX, 1), 0)
    row_mask = (rows < count).astype(F32)
    loads[0].wait()
    x_ref[0] = (crop_ref[...].astype(F32) * row_mask).astype(BF16)

    lane_block = lax.broadcasted_iota(jnp.int32, (OWN, 128), 1) >> 5
    mine = pl.ds(pl.multiple_of(OWN * fs, OWN), OWN)
    loads[1].wait()
    for g in range(TILES):
        tile = jnp.zeros((OWN, 128), F32)
        for j in range(4):
            if 4 * g + j < TAPS:
                tap = weight_ref[4 * g + j].astype(F32)
                tap = pltpu.roll(tap, lax.rem(32 * (j - q) + 128, 128), 1)
                tile = jnp.where(lane_block == j, tap, tile)
        wg_ref[mine, pl.ds(128 * g, 128)] = tile.astype(BF16)

    for load in loads[2:]:
        load.wait()
    ct_ref[...] = cot_ref[...].astype(F32).T.astype(BF16)
    bias_rows = lax.broadcasted_iota(jnp.int32, (8, OUTS), 0)
    bias_row = jnp.sum(jnp.where(bias_rows == bucket, bias_ref[...], 0.0), axis=0, keepdims=True)
    meta_ref[0] = jnp.where(bias_rows == 0, bias_row, count.astype(F32))

    pl.semaphore_wait(barrier, greeted)
    pending = []

    def send_block(src, dst, send, recv, k):
        copy = pltpu.make_async_remote_copy(
            src_ref=src, dst_ref=dst, send_sem=send.at[k - 1], recv_sem=recv.at[k - 1],
            device_id=member(k), device_id_type=MESH,
        )
        copy.start()
        pending.append(copy.wait_send)

    chips_x = peers // 2
    sibling = (dp, fs + 1 - 2 * lax.rem(fs, 2))

    def piece(k):
        return pl.ds(pl.multiple_of(OWN * lax.rem(fs + 2 * k, peers), OWN), OWN)

    def send_piece(rows, index, device):
        copy = pltpu.make_async_remote_copy(
            src_ref=wg_ref.at[rows, :], dst_ref=wg_ref.at[rows, :],
            send_sem=w_send.at[index], recv_sem=w_recv.at[index], device_id=device, device_id_type=MESH,
        )
        copy.start()
        pending.append(copy.wait_send)

    for k in range(1, chips_x):
        send_piece(mine, k - 1, along(2 * k))
    send_piece(mine, chips_x - 1, sibling)
    for k in range(1, 4):
        send_block(meta_ref.at[0], meta_ref.at[k], m_send, m_recv, k)
    for k in (1, 3, 2):
        send_block(x_ref.at[0], x_ref.at[k], x_send, x_recv, k)

    for k in range(1, 4):
        to = pl.ds(pl.multiple_of(QUARTER * (q ^ k), QUARTER), QUARTER)
        send_block(ct_ref.at[to, :], c4_ref.at[k], c_send, c_recv, k)
    tell(0, rounds[0])
    quarter = pl.ds(pl.multiple_of(QUARTER * q, QUARTER), QUARTER)
    c4_ref[0] = ct_ref[quarter, :]

    for k in range(1, 4):
        wait_bytes(meta_ref.at[k], m_recv.at[k - 1])
    table = jnp.concatenate(
        [meta_ref[k, 0:1, :] for k in range(4)]
        + [gain_ref[...], shift_ref[...], jnp.zeros((122, OUTS), F32)],
        axis=0,
    )
    par_ref[...] = table.T
    hear(0, rounds[0])
    tell(1, rounds[1])
    params = par_ref[quarter, :]
    param_lane = lax.broadcasted_iota(jnp.int32, (QUARTER, OUTS), 1)

    def column(index):
        return jnp.sum(jnp.where(param_lane == index, params, 0.0), axis=1, keepdims=True)

    gain = column(4)
    shift = column(5)

    for k in range(1, chips_x):
        source = piece(chips_x - k)
        wait_bytes(wg_ref.at[source, :], w_recv.at[k - 1])
        send_piece(source, chips_x - 1 + k, sibling)
    for k in range(chips_x):
        wait_bytes(wg_ref.at[mine, :], w_recv.at[chips_x - 1 + k])
    for g in range(TILES):
        wt_ref[pl.ds(128 * g, 128), :] = wg_ref[:, pl.ds(128 * g, 128)].astype(F32).T.astype(BF16)

    zf, yf, xf = lane_fields()
    reach = {
        (axis, offset): inside(offset, field, cells).astype(F32)
        for axis, field, cells in (("z", zf, 4), ("y", yf, 8), ("x", xf, 8))
        for offset in (-1, 1)
    }

    def moved(value, axis, offset, step):
        if offset == 0:
            return value
        rolled = pltpu.roll(value, (-offset * step) % VOX, 1)
        return rolled * reach[axis, offset]

    def group_sum(value):
        grouped = value.reshape(QUARTER // 8, 8, VOX)
        total = jnp.sum(jnp.sum(grouped, axis=2, keepdims=True), axis=1, keepdims=True)
        return total


    lane = lax.broadcasted_iota(jnp.int32, (1, VOX), 1).astype(F32)

    def spread(total):
        return jnp.broadcast_to(total, (QUARTER // 8, 8, VOX)).reshape(QUARTER, VOX)

    def normalize(m, pre):
        cells = meta_ref[m][1:2, 0:1]
        mask = (lane < cells).astype(F32)
        inverse = (1.0 / (cells * 8.0)).reshape(1, 1, 1)
        mean = spread(group_sum(pre * mask) * inverse)
        centered = pre - mean
        variance = group_sum(centered * centered * mask) * inverse
        scale = spread(lax.rsqrt(variance + EPSILON))
        normed = centered * scale
        value = normed * gain + shift + column(m)
        sig = 1.0 / (1.0 + jnp.exp(-value))
        acts_ref[m] = (value * sig * mask).astype(BF16)
        d_normed = c4_ref[m].astype(F32) * mask * (sig * (1.0 + value * (1.0 - sig))) * gain
        mean_d = spread(group_sum(d_normed) * inverse)
        mean_dn = spread(group_sum(d_normed * normed) * inverse)
        grad = scale * (d_normed - mask * (mean_d + normed * mean_dn))
        return grad.astype(BF16).astype(F32)

    def crops_of(pair, between=None):
        xts, pre, sum_z, sum_y, grads = {}, {}, {}, {}, {}
        for m in pair:
            if m > 0:
                wait_bytes(x_ref.at[m], x_recv.at[m - 1])
        for m in pair:
            xts[m] = x_ref[m].astype(F32).T.astype(BF16)
            xt_ref[m] = xts[m]
            pre[m] = jnp.zeros((QUARTER, VOX), F32)
        for g in range(TILES):
            for m in pair:
                product = jnp.dot(wt_ref[pl.ds(128 * g, 128), :], xts[m], preferred_element_type=F32)
                for j in range(4):
                    t = 4 * g + j
                    if t >= TAPS:
                        continue
                    a, b, e = t // 9 - 1, t // 3 % 3 - 1, t % 3 - 1
                    part = moved(product[32 * j : 32 * j + 32], "x", e, 1)
                    sum_y[m] = part if e == -1 else sum_y[m] + part
                    if e == 1:
                        part = moved(sum_y[m], "y", b, 8)
                        sum_z[m] = part if b == -1 else sum_z[m] + part
                        if b == 1:
                            pre[m] = pre[m] + moved(sum_z[m], "z", a, 64)
        if between is not None:
            between()
        for m in pair:
            if m > 0:
                wait_bytes(c4_ref.at[m], c_recv.at[m - 1])
        for m in pair:
            grads[m] = normalize(m, pre[m])
        for a in range(-1, 2):
            grad_a = {m: moved(grads[m], "z", -a, 64) for m in pair}
            for b in range(-1, 2):
                grad_ab = {m: moved(grad_a[m], "y", -b, 8) for m in pair}
                for e in range(-1, 2):
                    t = 9 * (a + 1) + 3 * (b + 1) + e + 1
                    for m in pair:
                        g_ref[m, pl.ds(32 * t, 32), :] = moved(grad_ab[m], "x", -e, 1).astype(BF16)
        for m in pair:
            g_ref[m, pl.ds(32 * TAPS, 32), :] = jnp.zeros((32, VOX), BF16)

    def gradient(pair, lanes, width):
        total = None
        for m in pair:
            term = lax.dot_general(
                xt_ref[m], g_ref[m, lanes, :], (((1,), (1,)), ((), ())), preferred_element_type=F32
            )
            total = term if total is None else total + term
        return total.reshape(chips_x, 2, OWN, width)

    def second_round():
        hear(1, rounds[1])
        tell(2, rounds[2])

    crops_of((0, 1), second_round)
    for start, width in CHUNKS:
        lanes = pl.ds(start, width)
        dwf_ref[:, :, :, lanes] = gradient((0, 1), lanes, width)
    crops_of((2, 3))
    for k in range(1, 4):
        copy = pltpu.make_async_remote_copy(
            src_ref=acts_ref.at[k], dst_ref=actr_ref.at[quarter, :],
            send_sem=a_send.at[k - 1], recv_sem=a_recv.at[k - 1],
            device_id=member(k), device_id_type=MESH,
        )
        copy.start()
        pending.append(copy.wait_send)
    actr_ref[quarter, :] = acts_ref[0]

    side_c = lax.rem(fs, 2)
    chip_x = fs // 2
    for index, (start, width) in enumerate(CHUNKS):
        lanes = pl.ds(start, width)
        dwf_ref[:, :, :, lanes] += gradient((2, 3), lanes, width)
        copy = pltpu.make_async_remote_copy(
            src_ref=dwf_ref.at[:, 1 - side_c, :, lanes], dst_ref=d0r_ref.at[:, :, lanes],
            send_sem=d0_send.at[index], recv_sem=d0_recv.at[index], device_id=sibling, device_id_type=MESH,
        )
        copy.start()
        pending.append(copy.wait_send)
    hear(2, rounds[2])
    tell(3, rounds[3])
    for index, (start, width) in enumerate(CHUNKS):
        lanes = pl.ds(start, width)
        wait_bytes(d0r_ref.at[:, :, lanes], d0_recv.at[index])
        total = dwf_ref[:, side_c, :, lanes] + d0r_ref[:, :, lanes]
        d0r_ref[:, :, lanes] = total
        d1s_ref[:, :, lanes] = total
        for k in sorted(range(1, chips_x), key=lambda k: -min(k, chips_x - k)):
            copy = pltpu.make_async_remote_copy(
                src_ref=d1s_ref.at[lax.rem(chip_x + k, chips_x), :, lanes], dst_ref=d1r_ref.at[k - 1, :, lanes],
                send_sem=d1_send.at[index, k - 1], recv_sem=d1_recv.at[index],
                device_id=along(2 * k), device_id_type=MESH,
            )
            copy.start()
            pending.append(copy.wait_send)
    hear(3, rounds[3])

    def owner(u):
        return u // per_row, places[u % per_row // per_dev]

    for index, (start, width) in enumerate(CHUNKS):
        lanes = pl.ds(start, width)
        if chips_x > 1:
            wait_bytes(d1r_ref.at[:, :, lanes], d1_recv.at[index])
        total = d0r_ref[chip_x, :, lanes]
        for k in range(1, chips_x):
            total = total + d1r_ref[k - 1, :, lanes].astype(F32)
        for g in range(start // 128, (start + width) // 128):
            for h in range(2):
                u = 2 * g + h
                at = 128 * g - start
                s_ref[u] = total[16 * h : 16 * h + 16, at : at + 128].astype(BF16)
                oy, oz = owner(u)
                away = jnp.logical_or(yp != oy, zp != oz)
                slot = lax.rem(yp - oy + nyp, nyp) * nzp + lax.rem(zp - oz + nzp, nzp) - 1
                copy = pltpu.make_async_remote_copy(
                    src_ref=s_ref.at[u],
                    dst_ref=r2_ref.at[u % per_dev, jnp.maximum(slot, 0)],
                    send_sem=d2_send.at[u], recv_sem=d2_recv.at[u % per_dev],
                    device_id=plane(2 * oy + qy, 2 * oz + qz), device_id_type=MESH,
                )
                pl.when(away)(copy.start)
                pending.append(functools.partial(pl.when(away), copy.wait_send))

    owns = functools.reduce(jnp.logical_or, [zp == place for place in places])
    my_spot = sum(jnp.where(zp == place, spot, 0) for spot, place in enumerate(places))
    first = yp * per_row + my_spot * per_dev
    owns = jnp.logical_and(owns, first < REAL)
    own_units = f_ref.at[pl.ds(first, per_dev), qy, qz]

    def unit_copy(target):
        return pltpu.make_async_remote_copy(
            src_ref=own_units, dst_ref=own_units,
            send_sem=e1_send.at[target], recv_sem=e1_recv.at[my_spot, qz],
            device_id=plane(y, target), device_id_type=MESH,
        )

    @pl.when(owns)
    def _():
        for i in range(per_dev):
            u = first + i

            @pl.when(u < REAL)
            def _():
                wait_bytes(r2_ref.at[i], d2_recv.at[i])
                total = s_ref[u].astype(F32)
                for k in range(nyp * nzp - 1):
                    total = total + r2_ref[i, k].astype(F32)
                f_ref[u, qy, qz] = total.astype(BF16)

            @pl.when(u >= REAL)
            def _():
                f_ref[u, qy, qz] = jnp.zeros((16, 128), BF16)

        for target in range(nz):
            pl.when(z != target)(unit_copy(target).start)

    def sent():
        @pl.when(owns)
        def _():
            for target in range(nz):
                pl.when(z != target)(unit_copy(target).wait_send)

    pending.append(sent)

    for k in range(1, 4):
        theirs = pl.ds(pl.multiple_of(QUARTER * (q ^ k), QUARTER), QUARTER)
        wait_bytes(actr_ref.at[theirs, :], a_recv.at[k - 1])
    act_ref[...] = actr_ref[...].astype(F32).T.astype(BF16)


    def start_of(row, spot):
        return (row // 2) * per_row + spot * per_dev

    def row_units(row, spot):
        return f_ref.at[pl.ds(start_of(row, spot), per_dev), lax.rem(row, 2)]

    def row_copy(spot, k):
        return pltpu.make_async_remote_copy(
            src_ref=row_units(y, spot), dst_ref=row_units(y, spot),
            send_sem=e2_send.at[spot, k - 1], recv_sem=e2_recv.at[spot, k - 1],
            device_id=plane(lax.rem(y + k, ny), z), device_id_type=MESH,
        )

    far_first = sorted(range(1, ny), key=lambda k: -min(k, ny - k))

    def pass_on(spot, at):
        @pl.when(start_of(y, spot) < REAL)
        def _():
            for side in range(2):
                @pl.when(jnp.logical_not(jnp.logical_and(zp == at, qz == side)))
                def _():
                    units = f_ref.at[pl.ds(start_of(y, spot), per_dev), qy, side]
                    wait_bytes(units, e1_recv.at[spot, side])

            for k in far_first:
                row_copy(spot, k).start()

    def row_sent():
        for spot in range(spots):
            @pl.when(start_of(y, spot) < REAL)
            def _():
                for k in range(1, ny):
                    row_copy(spot, k).wait_send()

    pending.append(row_sent)
    for spot, place in enumerate(places):
        pass_on(spot, place)
    for k in range(1, ny):
        from_row = lax.rem(y + ny - k, ny)
        for spot in range(spots):
            @pl.when(start_of(from_row, spot) < REAL)
            def _():
                wait_bytes(row_units(from_row, spot), e2_recv.at[spot, k - 1])


    block16 = lax.broadcasted_iota(jnp.int32, (16, 128), 1) >> 5
    for g in range(TILES):
        for h in range(2):
            quarters = [f_ref[2 * g + h, p // 2, p % 2].astype(F32) for p in range(4)]
            for j in range(4):
                t = 4 * g + j
                if t >= TAPS:
                    continue
                line = jnp.zeros((16, 128), F32)
                for p in range(4):
                    turned = quarters[p] if p == j else pltpu.roll(quarters[p], (32 * (p - j)) % 128, 1)
                    line = jnp.where(block16 == p, turned, line)
                grad_ref[t, 16 * h : 16 * h + 16, :] = line
    for wait in pending:
        wait()

def body(geometry, crops, weight, bucket_bias, norm_gain, norm_shift, bucket_ids, valid_counts, cotangent):
    ny, nz, peers = geometry
    nyp, nzp = ny // 2, nz // 2
    per_row = UNITS // nyp
    places = SPOTS.get(nzp, tuple(range(min(per_row, nzp, 4))))
    spots = len(places)
    per_dev = per_row // spots
    chans = OWN * peers
    others = max(1, peers - 1)
    smem = pl.BlockSpec(memory_space=pltpu.SMEM)
    vmem = pl.BlockSpec(memory_space=pltpu.VMEM)
    dma = pltpu.SemaphoreType.DMA
    def hold(x):
        return pltpu.with_memory_space_constraint(x, pltpu.HBM)

    activated, grad = pl.pallas_call(
        functools.partial(kernel, geometry),
        out_shape=(
            jax.ShapeDtypeStruct((VOX, OUTS), BF16),
            jax.ShapeDtypeStruct((TAPS, OWN, OUTS), F32),
        ),
        in_specs=[smem, smem] + [pl.BlockSpec(memory_space=pltpu.HBM)] * 6,
        out_specs=(vmem, vmem),
        scratch_shapes=[
            pltpu.VMEM((VOX, chans), BF16),
            pltpu.VMEM((TAPS, OWN, OUTS), BF16),
            pltpu.VMEM(bucket_bias.shape, F32),
            pltpu.VMEM((1, OUTS), F32),
            pltpu.VMEM((1, OUTS), F32),
            pltpu.VMEM((VOX, OUTS), BF16),
            dma((6,)),
            pltpu.VMEM((4, VOX, chans), BF16),
            pltpu.VMEM((4, chans, VOX), BF16),
            pltpu.VMEM((chans, COLS), BF16),
            pltpu.VMEM((COLS, chans), BF16),
            pltpu.VMEM((OUTS, VOX), BF16),
            pltpu.VMEM((4, QUARTER, VOX), BF16),
            pltpu.VMEM((4, 8, OUTS), F32),
            pltpu.VMEM((OUTS, OUTS), F32),
            pltpu.VMEM((4, COLS, VOX), BF16),
            pltpu.VMEM((peers // 2, 2, OWN, COLS), F32),
            pltpu.VMEM((peers // 2, OWN, COLS), F32),
            pltpu.VMEM((peers // 2, OWN, COLS), F32),
            pltpu.VMEM((max(1, peers // 2 - 1), OWN, COLS), F32),
            pltpu.VMEM((REAL, 16, 128), BF16),
            pltpu.VMEM((per_dev, max(1, nyp * nzp - 1), 16, 128), BF16),
            pltpu.VMEM((UNITS, 2, 2, 16, 128), BF16),
            pltpu.VMEM((4, QUARTER, VOX), BF16),
            pltpu.VMEM((OUTS, VOX), BF16),
            pltpu.SemaphoreType.REGULAR((4,)),
            dma((others,)), dma((others,)),
            dma((3,)), dma((3,)),
            dma((3,)), dma((3,)),
            dma((3,)), dma((3,)),
            dma((3,)), dma((3,)),
            dma((len(CHUNKS),)), dma((len(CHUNKS),)),
            dma((len(CHUNKS), others)), dma((len(CHUNKS),)),
            dma((REAL,)), dma((per_dev,)),
            dma((nz,)), dma((spots, 2)),
            dma((spots, ny - 1)), dma((spots, ny - 1)),
        ],
        compiler_params=pltpu.CompilerParams(
            collective_id=0, has_side_effects=True, vmem_limit_bytes=40 * 1024 * 1024
        ),
    )(
        valid_counts, bucket_ids,
        hold(crops.reshape(VOX, chans)), hold(weight.transpose(1, 0, 2)), hold(bucket_bias),
        hold(norm_gain.reshape(1, OUTS)), hold(norm_shift.reshape(1, OUTS)), hold(cotangent.reshape(VOX, OUTS)),
    )
    return activated[None], grad.transpose(1, 0, 2)


def solution(mesh):
    chips = mesh.shape["dp"]
    ny = 8 if chips == 128 else 2
    geometry = (ny, chips // ny, mesh.shape["fsdp"])
    return jax.shard_map(
        functools.partial(body, geometry),
        mesh=mesh,
        in_specs=(
            P(("dp", "fsdp"), None, None, None, None),
            P("fsdp", None, None),
            P(),
            P(),
            P(),
            P(("dp", "fsdp")),
            P(("dp", "fsdp")),
            P(("dp", "fsdp"), None, None),
        ),
        out_specs=(P(("dp", "fsdp"), None, None), P("fsdp", None, None)),
        check_vma=False,
    )
```

```python
import functools

import jax
import jax.numpy as jnp
from jax import lax
from jax.experimental import pallas as pl
from jax.experimental.pallas import tpu as pltpu
from jax.sharding import PartitionSpec as P

MESH = pl.DeviceIdType.MESH
F32 = jnp.float32
BF16 = jnp.bfloat16

EPSILON = 1e-05
VOX = 256
OWN = 32
OUTS = 128
QUARTER = 32
TAPS = 27
TILES = 7
COLS = TILES * 128
UNITS = 16
REAL = 2 * TILES
SPOTS = {8: (7, 0, 6, 1)}
CHUNKS = ((0, 256), (256, 256), (512, 256), (768, 128))


def lane_fields():
    lane = lax.broadcasted_iota(jnp.int32, (8, VOX), 1)
    return lane >> 6, (lane >> 3) & 7, lane & 7


def inside(offset, field, cells):
    moved = field + offset
    return jnp.logical_and(moved >= 0, moved < cells)[0:1]


def wait_bytes(ref, sem):
    pltpu.make_async_copy(ref, ref, sem).wait()


def kernel(
    geometry,
    count_ref, bucket_ref, crop_hbm, weight_hbm, bias_hbm, gain_hbm, shift_hbm, cot_hbm,
    act_ref, grad_ref,
    crop_ref, weight_ref, bias_ref, gain_ref, shift_ref, cot_ref, in_sem,
    x_ref, xt_ref, wg_ref, wt_ref, ct_ref, c4_ref, meta_ref, par_ref,
    g_ref, dwf_ref, d0r_ref, d1s_ref, d1r_ref, s_ref, r2_ref, f_ref, acts_ref, actr_ref,
    told, w_send, w_recv, x_send, x_recv, c_send, c_recv, m_send, m_recv, a_send, a_recv,
    d0_send, d0_recv, d1_send, d1_recv, d2_send, d2_recv, e1_send, e1_recv, e2_send, e2_recv,
):
    ny, nz, peers = geometry
    nyp, nzp = ny // 2, nz // 2
    per_row = UNITS // nyp
    places = SPOTS.get(nzp, tuple(range(min(per_row, nzp, 4))))
    spots = len(places)
    per_dev = per_row // spots
    chans = OWN * peers

    dp = lax.axis_index("dp")
    fs = lax.axis_index("fsdp")
    y, z = dp // nz, dp % nz
    yp, zp, qy, qz = y // 2, z // 2, y % 2, z % 2
    q = qy * 2 + qz

    def plane(yy, zz):
        return (yy * nz + zz, fs)

    def along(k):
        return (dp, lax.rem(fs + k, peers))

    def member(k):
        return plane(2 * yp + (qy ^ (k >> 1)), 2 * zp + (qz ^ (k & 1)))

    loads = [
        pltpu.make_async_copy(src, dst, in_sem.at[index])
        for index, (src, dst) in enumerate((
            (crop_hbm, crop_ref), (weight_hbm, weight_ref), (cot_hbm, cot_ref),
            (bias_hbm, bias_ref), (gain_hbm, gain_ref), (shift_hbm, shift_ref),
        ))
    ]
    for load in loads:
        load.start()

    barrier = pltpu.get_barrier_semaphore()

    def greet(device):
        pl.semaphore_signal(barrier, inc=1, device_id=device, device_id_type=MESH)

    for k in range(1, peers):
        greet(along(k))
    for k in range(1, 4):
        greet(member(k))
    greeted = peers - 1 + 3

    def offsets(*pairs):
        return sorted({(a % nyp, b % nzp) for a, b in pairs} - {(0, 0)})

    beside = offsets((0, 1), (0, -1), (1, 0), (-1, 0))
    second = offsets((0, 2), (0, -2), (2, 0), (1, 1), (1, -1), (-1, 1), (-1, -1))
    along_z = offsets((0, 2), (0, -2))

    def block(a, b):
        return plane(2 * lax.rem(yp + a, nyp) + qy, 2 * lax.rem(zp + b, nzp) + qz)

    for a, b in beside:
        greet(block(a, b))
    greeted += len(beside)

    def tell(step, devices):
        for device in devices:
            pl.semaphore_signal(told.at[step], inc=1, device_id=device, device_id_type=MESH)

    def hear(step, devices):
        if devices:
            pl.semaphore_wait(told.at[step], len(devices))

    rounds = (
        [block(a, b) for a, b in beside],
        [block(a, b) for a, b in second],
        [block(a, b) for a, b in along_z],
        [member(k) for k in range(1, 4)],
    )

    count = count_ref[0]
    bucket = bucket_ref[0]
    rows = lax.broadcasted_iota(jnp.int32, (VOX, 1), 0)
    row_mask = (rows < count).astype(F32)
    loads[0].wait()
    x_ref[0] = (crop_ref[...].astype(F32) * row_mask).astype(BF16)

    lane_block = lax.broadcasted_iota(jnp.int32, (OWN, 128), 1) >> 5
    mine = pl.ds(pl.multiple_of(OWN * fs, OWN), OWN)
    loads[1].wait()
    for g in range(TILES):
        tile = jnp.zeros((OWN, 128), F32)
        for j in range(4):
            if 4 * g + j < TAPS:
                tap = weight_ref[4 * g + j].astype(F32)
                tap = pltpu.roll(tap, lax.rem(32 * (j - q) + 128, 128), 1)
                tile = jnp.where(lane_block == j, tap, tile)
        wg_ref[mine, pl.ds(128 * g, 128)] = tile.astype(BF16)

    for load in loads[2:]:
        load.wait()
    ct_ref[...] = cot_ref[...].astype(F32).T.astype(BF16)
    bias_rows = lax.broadcasted_iota(jnp.int32, (8, OUTS), 0)
    bias_row = jnp.sum(jnp.where(bias_rows == bucket, bias_ref[...], 0.0), axis=0, keepdims=True)
    meta_ref[0] = jnp.where(bias_rows == 0, bias_row, count.astype(F32))

    pl.semaphore_wait(barrier, greeted)
    pending = []

    def send_block(src, dst, send, recv, k):
        copy = pltpu.make_async_remote_copy(
            src_ref=src, dst_ref=dst, send_sem=send.at[k - 1], recv_sem=recv.at[k - 1],
            device_id=member(k), device_id_type=MESH,
        )
        copy.start()
        pending.append(copy.wait_send)

    chips_x = peers // 2
    sibling = (dp, fs + 1 - 2 * lax.rem(fs, 2))

    def piece(k):
        return pl.ds(pl.multiple_of(OWN * lax.rem(fs + 2 * k, peers), OWN), OWN)

    def send_piece(rows, index, device):
        copy = pltpu.make_async_remote_copy(
            src_ref=wg_ref.at[rows, :], dst_ref=wg_ref.at[rows, :],
            send_sem=w_send.at[index], recv_sem=w_recv.at[index], device_id=device, device_id_type=MESH,
        )
        copy.start()
        pending.append(copy.wait_send)

    for k in range(1, chips_x):
        send_piece(mine, k - 1, along(2 * k))
    send_piece(mine, chips_x - 1, sibling)
    for k in range(1, 4):
        send_block(meta_ref.at[0], meta_ref.at[k], m_send, m_recv, k)
    for k in (1, 3, 2):
        send_block(x_ref.at[0], x_ref.at[k], x_send, x_recv, k)

    for k in range(1, 4):
        to = pl.ds(pl.multiple_of(QUARTER * (q ^ k), QUARTER), QUARTER)
        send_block(ct_ref.at[to, :], c4_ref.at[k], c_send, c_recv, k)
    tell(0, rounds[0])
    quarter = pl.ds(pl.multiple_of(QUARTER * q, QUARTER), QUARTER)
    c4_ref[0] = ct_ref[quarter, :]

    for k in range(1, 4):
        wait_bytes(meta_ref.at[k], m_recv.at[k - 1])
    table = jnp.concatenate(
        [meta_ref[k, 0:1, :] for k in range(4)]
        + [gain_ref[...], shift_ref[...], jnp.zeros((122, OUTS), F32)],
        axis=0,
    )
    par_ref[...] = table.T
    hear(0, rounds[0])
    tell(1, rounds[1])
    params = par_ref[quarter, :]
    param_lane = lax.broadcasted_iota(jnp.int32, (QUARTER, OUTS), 1)

    def column(index):
        return jnp.sum(jnp.where(param_lane == index, params, 0.0), axis=1, keepdims=True)

    gain = column(4)
    shift = column(5)

    for k in range(1, chips_x):
        source = piece(chips_x - k)
        wait_bytes(wg_ref.at[source, :], w_recv.at[k - 1])
        send_piece(source, chips_x - 1 + k, sibling)
    for k in range(chips_x):
        wait_bytes(wg_ref.at[mine, :], w_recv.at[chips_x - 1 + k])
    for g in range(TILES):
        wt_ref[pl.ds(128 * g, 128), :] = wg_ref[:, pl.ds(128 * g, 128)].astype(F32).T.astype(BF16)

    zf, yf, xf = lane_fields()
    reach = {
        (axis, offset): inside(offset, field, cells).astype(F32)
        for axis, field, cells in (("z", zf, 4), ("y", yf, 8), ("x", xf, 8))
        for offset in (-1, 1)
    }

    def moved(value, axis, offset, step):
        if offset == 0:
            return value
        rolled = pltpu.roll(value, (-offset * step) % VOX, 1)
        return rolled * reach[axis, offset]

    def group_sum(value):
        grouped = value.reshape(QUARTER // 8, 8, VOX)
        total = jnp.sum(jnp.sum(grouped, axis=2, keepdims=True), axis=1, keepdims=True)
        return total


    lane = lax.broadcasted_iota(jnp.int32, (1, VOX), 1).astype(F32)

    def spread(total):
        return jnp.broadcast_to(total, (QUARTER // 8, 8, VOX)).reshape(QUARTER, VOX)

    def normalize(m, pre):
        cells = meta_ref[m][1:2, 0:1]
        mask = (lane < cells).astype(F32)
        inverse = (1.0 / (cells * 8.0)).reshape(1, 1, 1)
        mean = spread(group_sum(pre * mask) * inverse)
        centered = pre - mean
        variance = group_sum(centered * centered * mask) * inverse
        scale = spread(lax.rsqrt(variance + EPSILON))
        normed = centered * scale
        value = normed * gain + shift + column(m)
        sig = 1.0 / (1.0 + jnp.exp(-value))
        acts_ref[m] = (value * sig * mask).astype(BF16)
        d_normed = c4_ref[m].astype(F32) * mask * (sig * (1.0 + value * (1.0 - sig))) * gain
        mean_d = spread(group_sum(d_normed) * inverse)
        mean_dn = spread(group_sum(d_normed * normed) * inverse)
        grad = scale * (d_normed - mask * (mean_d + normed * mean_dn))
        return grad.astype(BF16).astype(F32)

    def crops_of(pair, between=None):
        xts, pre, sum_z, sum_y, grads = {}, {}, {}, {}, {}
        for m in pair:
            if m > 0:
                wait_bytes(x_ref.at[m], x_recv.at[m - 1])
        for m in pair:
            xts[m] = x_ref[m].astype(F32).T.astype(BF16)
            xt_ref[m] = xts[m]
            pre[m] = jnp.zeros((QUARTER, VOX), F32)
        for g in range(TILES):
            for m in pair:
                product = jnp.dot(wt_ref[pl.ds(128 * g, 128), :], xts[m], preferred_element_type=F32)
                for j in range(4):
                    t = 4 * g + j
                    if t >= TAPS:
                        continue
                    a, b, e = t // 9 - 1, t // 3 % 3 - 1, t % 3 - 1
                    part = moved(product[32 * j : 32 * j + 32], "x", e, 1)
                    sum_y[m] = part if e == -1 else sum_y[m] + part
                    if e == 1:
                        part = moved(sum_y[m], "y", b, 8)
                        sum_z[m] = part if b == -1 else sum_z[m] + part
                        if b == 1:
                            pre[m] = pre[m] + moved(sum_z[m], "z", a, 64)
        if between is not None:
            between()
        for m in pair:
            if m > 0:
                wait_bytes(c4_ref.at[m], c_recv.at[m - 1])
        for m in pair:
            grads[m] = normalize(m, pre[m])
        for a in range(-1, 2):
            grad_a = {m: moved(grads[m], "z", -a, 64) for m in pair}
            for b in range(-1, 2):
                grad_ab = {m: moved(grad_a[m], "y", -b, 8) for m in pair}
                for e in range(-1, 2):
                    t = 9 * (a + 1) + 3 * (b + 1) + e + 1
                    for m in pair:
                        g_ref[m, pl.ds(32 * t, 32), :] = moved(grad_ab[m], "x", -e, 1).astype(BF16)
        for m in pair:
            g_ref[m, pl.ds(32 * TAPS, 32), :] = jnp.zeros((32, VOX), BF16)

    def gradient(pair, lanes, width):
        total = None
        for m in pair:
            term = lax.dot_general(
                xt_ref[m], g_ref[m, lanes, :], (((1,), (1,)), ((), ())), preferred_element_type=F32
            )
            total = term if total is None else total + term
        return total.reshape(chips_x, 2, OWN, width)

    def second_round():
        hear(1, rounds[1])
        tell(2, rounds[2])

    crops_of((0, 1), second_round)
    for start, width in CHUNKS:
        lanes = pl.ds(start, width)
        dwf_ref[:, :, :, lanes] = gradient((0, 1), lanes, width)
    crops_of((2, 3))
    for k in range(1, 4):
        copy = pltpu.make_async_remote_copy(
            src_ref=acts_ref.at[k], dst_ref=actr_ref.at[quarter, :],
            send_sem=a_send.at[k - 1], recv_sem=a_recv.at[k - 1],
            device_id=member(k), device_id_type=MESH,
        )
        copy.start()
        pending.append(copy.wait_send)
    actr_ref[quarter, :] = acts_ref[0]

    side_c = lax.rem(fs, 2)
    chip_x = fs // 2
    for index, (start, width) in enumerate(CHUNKS):
        lanes = pl.ds(start, width)
        dwf_ref[:, :, :, lanes] += gradient((2, 3), lanes, width)
        copy = pltpu.make_async_remote_copy(
            src_ref=dwf_ref.at[:, 1 - side_c, :, lanes], dst_ref=d0r_ref.at[:, :, lanes],
            send_sem=d0_send.at[index], recv_sem=d0_recv.at[index], device_id=sibling, device_id_type=MESH,
        )
        copy.start()
        pending.append(copy.wait_send)
    hear(2, rounds[2])
    tell(3, rounds[3])
    for index, (start, width) in enumerate(CHUNKS):
        lanes = pl.ds(start, width)
        wait_bytes(d0r_ref.at[:, :, lanes], d0_recv.at[index])
        total = dwf_ref[:, side_c, :, lanes] + d0r_ref[:, :, lanes]
        d0r_ref[:, :, lanes] = total
        d1s_ref[:, :, lanes] = total
        for k in sorted(range(1, chips_x), key=lambda k: -min(k, chips_x - k)):
            copy = pltpu.make_async_remote_copy(
                src_ref=d1s_ref.at[lax.rem(chip_x + k, chips_x), :, lanes], dst_ref=d1r_ref.at[k - 1, :, lanes],
                send_sem=d1_send.at[index, k - 1], recv_sem=d1_recv.at[index],
                device_id=along(2 * k), device_id_type=MESH,
            )
            copy.start()
            pending.append(copy.wait_send)
    hear(3, rounds[3])

    def owner(u):
        return u // per_row, places[u % per_row // per_dev]

    for index, (start, width) in enumerate(CHUNKS):
        lanes = pl.ds(start, width)
        if chips_x > 1:
            wait_bytes(d1r_ref.at[:, :, lanes], d1_recv.at[index])
        total = d0r_ref[chip_x, :, lanes]
        for k in range(1, chips_x):
            total = total + d1r_ref[k - 1, :, lanes].astype(F32)
        for g in range(start // 128, (start + width) // 128):
            for h in range(2):
                u = 2 * g + h
                at = 128 * g - start
                s_ref[u] = total[16 * h : 16 * h + 16, at : at + 128].astype(BF16)
                oy, oz = owner(u)
                away = jnp.logical_or(yp != oy, zp != oz)
                slot = lax.rem(yp - oy + nyp, nyp) * nzp + lax.rem(zp - oz + nzp, nzp) - 1
                copy = pltpu.make_async_remote_copy(
                    src_ref=s_ref.at[u],
                    dst_ref=r2_ref.at[u % per_dev, jnp.maximum(slot, 0)],
                    send_sem=d2_send.at[u], recv_sem=d2_recv.at[u % per_dev],
                    device_id=plane(2 * oy + qy, 2 * oz + qz), device_id_type=MESH,
                )
                pl.when(away)(copy.start)
                pending.append(functools.partial(pl.when(away), copy.wait_send))

    owns = functools.reduce(jnp.logical_or, [zp == place for place in places])
    my_spot = sum(jnp.where(zp == place, spot, 0) for spot, place in enumerate(places))
    first = yp * per_row + my_spot * per_dev
    owns = jnp.logical_and(owns, first < REAL)
    own_units = f_ref.at[pl.ds(first, per_dev), qy, qz]

    def unit_copy(target):
        return pltpu.make_async_remote_copy(
            src_ref=own_units, dst_ref=own_units,
            send_sem=e1_send.at[target], recv_sem=e1_recv.at[my_spot, qz],
            device_id=plane(y, target), device_id_type=MESH,
        )

    @pl.when(owns)
    def _():
        for i in range(per_dev):
            u = first + i

            @pl.when(u < REAL)
            def _():
                wait_bytes(r2_ref.at[i], d2_recv.at[i])
                total = s_ref[u].astype(F32)
                for k in range(nyp * nzp - 1):
                    total = total + r2_ref[i, k].astype(F32)
                f_ref[u, qy, qz] = total.astype(BF16)

            @pl.when(u >= REAL)
            def _():
                f_ref[u, qy, qz] = jnp.zeros((16, 128), BF16)

        for target in range(nz):
            pl.when(z != target)(unit_copy(target).start)

    def sent():
        @pl.when(owns)
        def _():
            for target in range(nz):
                pl.when(z != target)(unit_copy(target).wait_send)

    pending.append(sent)

    for k in range(1, 4):
        theirs = pl.ds(pl.multiple_of(QUARTER * (q ^ k), QUARTER), QUARTER)
        wait_bytes(actr_ref.at[theirs, :], a_recv.at[k - 1])
    act_ref[...] = actr_ref[...].astype(F32).T.astype(BF16)


    def start_of(row, spot):
        return (row // 2) * per_row + spot * per_dev

    def row_units(row, spot):
        return f_ref.at[pl.ds(start_of(row, spot), per_dev), lax.rem(row, 2)]

    def row_copy(spot, k):
        return pltpu.make_async_remote_copy(
            src_ref=row_units(y, spot), dst_ref=row_units(y, spot),
            send_sem=e2_send.at[spot, k - 1], recv_sem=e2_recv.at[spot, k - 1],
            device_id=plane(lax.rem(y + k, ny), z), device_id_type=MESH,
        )

    far_first = sorted(range(1, ny), key=lambda k: -min(k, ny - k))

    def pass_on(spot, at):
        @pl.when(start_of(y, spot) < REAL)
        def _():
            for side in range(2):
                @pl.when(jnp.logical_not(jnp.logical_and(zp == at, qz == side)))
                def _():
                    units = f_ref.at[pl.ds(start_of(y, spot), per_dev), qy, side]
                    wait_bytes(units, e1_recv.at[spot, side])

            for k in far_first:
                row_copy(spot, k).start()

    def row_sent():
        for spot in range(spots):
            @pl.when(start_of(y, spot) < REAL)
            def _():
                for k in range(1, ny):
                    row_copy(spot, k).wait_send()

    pending.append(row_sent)
    for spot, place in enumerate(places):
        pass_on(spot, place)
    for k in range(1, ny):
        from_row = lax.rem(y + ny - k, ny)
        for spot in range(spots):
            @pl.when(start_of(from_row, spot) < REAL)
            def _():
                wait_bytes(row_units(from_row, spot), e2_recv.at[spot, k - 1])


    block16 = lax.broadcasted_iota(jnp.int32, (16, 128), 1) >> 5
    for g in range(TILES):
        for h in range(2):
            quarters = [f_ref[2 * g + h, p // 2, p % 2].astype(F32) for p in range(4)]
            for j in range(4):
                t = 4 * g + j
                if t >= TAPS:
                    continue
                line = jnp.zeros((16, 128), F32)
                for p in range(4):
                    turned = quarters[p] if p == j else pltpu.roll(quarters[p], (32 * (p - j)) % 128, 1)
                    line = jnp.where(block16 == p, turned, line)
                grad_ref[t, 16 * h : 16 * h + 16, :] = line
    for wait in pending:
        wait()

def body(geometry, crops, weight, bucket_bias, norm_gain, norm_shift, bucket_ids, valid_counts, cotangent):
    ny, nz, peers = geometry
    nyp, nzp = ny // 2, nz // 2
    per_row = UNITS // nyp
    places = SPOTS.get(nzp, tuple(range(min(per_row, nzp, 4))))
    spots = len(places)
    per_dev = per_row // spots
    chans = OWN * peers
    others = max(1, peers - 1)
    smem = pl.BlockSpec(memory_space=pltpu.SMEM)
    vmem = pl.BlockSpec(memory_space=pltpu.VMEM)
    dma = pltpu.SemaphoreType.DMA
    def hold(x):
        return pltpu.with_memory_space_constraint(x, pltpu.HBM)

    activated, grad = pl.pallas_call(
        functools.partial(kernel, geometry),
        out_shape=(
            jax.ShapeDtypeStruct((VOX, OUTS), BF16),
            jax.ShapeDtypeStruct((TAPS, OWN, OUTS), F32),
        ),
        in_specs=[smem, smem] + [pl.BlockSpec(memory_space=pltpu.HBM)] * 6,
        out_specs=(vmem, vmem),
        scratch_shapes=[
            pltpu.VMEM((VOX, chans), BF16),
            pltpu.VMEM((TAPS, OWN, OUTS), BF16),
            pltpu.VMEM(bucket_bias.shape, F32),
            pltpu.VMEM((1, OUTS), F32),
            pltpu.VMEM((1, OUTS), F32),
            pltpu.VMEM((VOX, OUTS), BF16),
            dma((6,)),
            pltpu.VMEM((4, VOX, chans), BF16),
            pltpu.VMEM((4, chans, VOX), BF16),
            pltpu.VMEM((chans, COLS), BF16),
            pltpu.VMEM((COLS, chans), BF16),
            pltpu.VMEM((OUTS, VOX), BF16),
            pltpu.VMEM((4, QUARTER, VOX), BF16),
            pltpu.VMEM((4, 8, OUTS), F32),
            pltpu.VMEM((OUTS, OUTS), F32),
            pltpu.VMEM((4, COLS, VOX), BF16),
            pltpu.VMEM((peers // 2, 2, OWN, COLS), F32),
            pltpu.VMEM((peers // 2, OWN, COLS), F32),
            pltpu.VMEM((peers // 2, OWN, COLS), F32),
            pltpu.VMEM((max(1, peers // 2 - 1), OWN, COLS), F32),
            pltpu.VMEM((REAL, 16, 128), BF16),
            pltpu.VMEM((per_dev, max(1, nyp * nzp - 1), 16, 128), BF16),
            pltpu.VMEM((UNITS, 2, 2, 16, 128), BF16),
            pltpu.VMEM((4, QUARTER, VOX), BF16),
            pltpu.VMEM((OUTS, VOX), BF16),
            pltpu.SemaphoreType.REGULAR((4,)),
            dma((others,)), dma((others,)),
            dma((3,)), dma((3,)),
            dma((3,)), dma((3,)),
            dma((3,)), dma((3,)),
            dma((3,)), dma((3,)),
            dma((len(CHUNKS),)), dma((len(CHUNKS),)),
            dma((len(CHUNKS), others)), dma((len(CHUNKS),)),
            dma((REAL,)), dma((per_dev,)),
            dma((nz,)), dma((spots, 2)),
            dma((spots, ny - 1)), dma((spots, ny - 1)),
        ],
        compiler_params=pltpu.CompilerParams(
            collective_id=0, has_side_effects=True, vmem_limit_bytes=40 * 1024 * 1024
        ),
    )(
        valid_counts, bucket_ids,
        hold(crops.reshape(VOX, chans)), hold(weight.transpose(1, 0, 2)), hold(bucket_bias),
        hold(norm_gain.reshape(1, OUTS)), hold(norm_shift.reshape(1, OUTS)), hold(cotangent.reshape(VOX, OUTS)),
    )
    return activated[None], grad.transpose(1, 0, 2)


def solution(mesh):
    chips = mesh.shape["dp"]
    ny = 8 if chips == 128 else 2
    geometry = (ny, chips // ny, mesh.shape["fsdp"])
    return jax.shard_map(
        functools.partial(body, geometry),
        mesh=mesh,
        in_specs=(
            P(("dp", "fsdp"), None, None, None, None),
            P("fsdp", None, None),
            P(),
            P(),
            P(),
            P(("dp", "fsdp")),
            P(("dp", "fsdp")),
            P(("dp", "fsdp"), None, None),
        ),
        out_specs=(P(("dp", "fsdp"), None, None), P("fsdp", None, None)),
        check_vma=False,
    )
```
